32 devices in a mesh: chan: 4 (over x, core), tm: 2 (over y), stat: 4 (over z).
Axes of the slice: x: 2, y: 2, z: 4, core: 2. Of those that a mesh axis runs over, the one named last changes fastest.
Arguments:
- voltages: bfloat16 [8, 2, 512, 4096], P('chan', None, 'stat', 'tm'), may hold values from -6 to 6
- ref_index: int32 [8], replicated, may hold values from 0 to 511
- positions: int32 [4096], P('tm'), may hold values from 0 to 255
- aperture_weight: float32 [256], replicated, may hold values from 0.25 to 4
Outputs:
- coefficients: float32 [512, 8, 8, 128], P(('stat', 'tm', 'chan'))
The draws below stay inside these ranges and needn't reach their ends.
Inputs may be any that keep to these rules, and one draw needn't show every extreme that they name: Each entry of ref_index is a station number; entries may repeat. Each entry of positions is a raster cell index of the 16 x 16 raster.
All inputs are finite; a program needn't handle non-finite values.
Results may differ from the reference program's by a relative error of at most 0.0003.
Values may be sent and summed in bfloat16 or wider, within the bound.
No kernel may reach another device: no remote copies, remote signals or barrier semaphores. Data moves between devices by JAX's collectives and lax.ppermute only.
A program may use at most 128 MiB of HBM per device.

```python
import math
import jax
import jax.numpy as jnp
from jax import lax

STATIONS = 512
REFS = 8
RASTER = 16
ZERN = 64
TIME_DEV = 2048
CHANNELS = 8
TIME = 4096


def place_ends(array, rng, low, largest):
    longest = array.shape.index(max(array.shape))
    spots = []
    for shift in (0, 1):
        where = [jax.random.randint(jax.random.fold_in(rng, axis), (), 0, length) for axis, length in enumerate(array.shape)]
        where[longest] = (where[longest] + shift) % array.shape[longest]
        spots.append(tuple(where))
    return array.at[spots[0]].set(low).at[spots[1]].set(largest)


def spiked(result, rng, source, target, parts, factor):
    owner, partner = [(jnp.arange(result.shape[position]) // (result.shape[position] // parts)).reshape([-1 if axis == position else 1 for axis in range(result.ndim)]) for position in (source, target)]
    chosen = jax.random.permutation(rng, parts)[partner]
    strong = (owner == chosen) | (owner == (partner + parts // 2) % parts)
    return jnp.where(strong, factor * result, result)


def block_scale(own_key, dims, pieces, smallest, high):
    loudness, own = 1.0, jax.random.fold_in(own_key, 6)
    for axis_at, parts in pieces:
        heights = jnp.exp(jax.random.uniform(jax.random.fold_in(own, axis_at), (parts,), jnp.float32, smallest / len(pieces), high / len(pieces)))
        loudness = loudness * jnp.repeat(heights, dims[axis_at] // parts).reshape([-1 if axis == axis_at else 1 for axis in range(len(dims))])
    return loudness


def bell_draw_with(own_key, dims, scale, bound, cuts, heavy, held_as=jnp.bfloat16):
    values = scale * jax.random.normal(own_key, dims, jnp.float32)
    if cuts:
        values = values * block_scale(own_key, dims, cuts, -0.22, 0.18)
    return jnp.clip(spiked(values, jax.random.fold_in(own_key, 3), *heavy), -bound, bound).astype(held_as)


def setup_inputs(seed: int = 0) -> dict:
    streams_of = jax.random.split(jax.random.key(seed), 5)
    voltages = bell_draw_with(streams_of[0], (CHANNELS, 2, STATIONS, TIME), 1.0, 6.0, ((0, 4), (2, 4), (3, 2)), (3, 2, 4, 2.0))
    ref_index = place_ends(jax.random.randint(streams_of[1], (REFS,), 0, STATIONS), jax.random.fold_in(streams_of[1], 1), 0, STATIONS - 1).astype(jnp.int32)
    positions = place_ends(jax.random.randint(streams_of[2], (TIME,), 0, RASTER * RASTER), jax.random.fold_in(streams_of[2], 1), 0, (RASTER * RASTER) - 1).astype(jnp.int32)
    aperture_weight = jnp.clip(jnp.exp(jax.random.uniform(streams_of[3], (RASTER * RASTER,), jnp.float32, math.log(0.25), math.log(4.0))), 0.25, 4.0)
    return dict(voltages=voltages, ref_index=ref_index, positions=positions, aperture_weight=aperture_weight)


def zernike_table(raster, count):
    cell_ids = jnp.arange(raster * raster, dtype=jnp.int32)
    half_width = raster / 2.0
    grid_x = ((cell_ids // raster - raster // 2).astype(jnp.float32) + 0.5) / half_width
    grid_y = ((cell_ids % raster - raster // 2).astype(jnp.float32) + 0.5) / half_width
    radius_sq = grid_x * grid_x + grid_y * grid_y
    in_disk = jnp.where(radius_sq <= 1.0, 1.0, 0.0).astype(jnp.float32)
    columns = []
    degree = 0
    while len(columns) < count:
        for azimuth in range(-degree, degree + 1, 2):
            if len(columns) < count:
                order_abs = abs(azimuth)
                real_pow = jnp.ones_like(grid_x)
                imag_pow = jnp.zeros_like(grid_x)
                for power_i in range(order_abs):
                    real_pow, imag_pow = (real_pow * grid_x - imag_pow * grid_y, real_pow * grid_y + imag_pow * grid_x)
                radial = jnp.zeros_like(grid_x)
                for term_k in range((degree - order_abs) // 2 + 1):
                    weight_k = (-1) ** term_k * math.factorial(degree - term_k) / (math.factorial(term_k) * math.factorial((degree + order_abs) // 2 - term_k) * math.factorial((degree - order_abs) // 2 - term_k))
                    radial = radial + jnp.float32(weight_k) * radius_sq ** ((degree - 2 * term_k - order_abs) // 2)
                if azimuth > 0:
                    column = radial * real_pow * jnp.float32(math.sqrt(2.0 * (degree + 1)))
                elif azimuth < 0:
                    column = radial * imag_pow * jnp.float32(math.sqrt(2.0 * (degree + 1)))
                else:
                    column = radial * jnp.float32(math.sqrt(degree + 1.0))
                columns.append(column * in_disk)
        degree += 1
    return jnp.stack(columns, axis=1)

def dft_real():
    cell_ids = jnp.arange(RASTER * RASTER, dtype=jnp.int32)
    row_coord = cell_ids // RASTER - RASTER // 2
    col_coord = cell_ids % RASTER - RASTER // 2
    phases = (row_coord[:, None] * row_coord[None, :] + col_coord[:, None] * col_coord[None, :]) % RASTER
    angles = phases.astype(jnp.float32) * jnp.float32(2.0 * math.pi / RASTER)
    cosine = jnp.cos(angles)
    sine_part = jnp.sin(angles)
    upper_rows = jnp.concatenate([cosine, sine_part], axis=1)
    bottom = jnp.concatenate([-sine_part, cosine], axis=1)
    return jnp.concatenate([upper_rows, bottom], axis=0)

def fit_tables(aperture_weight):
    zernike = zernike_table(RASTER, ZERN)
    weighted = zernike * aperture_weight[:, None]
    gram_matrix = jnp.dot(zernike.T, weighted, precision=lax.Precision.HIGHEST)
    factor = jnp.linalg.cholesky(gram_matrix)
    return (weighted, factor)

def finish(beam, weighted, factor, dft_table):
    leading = beam.shape[:3]
    flat_maps = beam.reshape(leading + (2 * RASTER * RASTER,))
    aperture = jnp.dot(flat_maps, dft_table.T, precision=lax.Precision.HIGHEST)
    aperture = aperture.reshape(leading + (2, RASTER * RASTER))
    projected = jnp.dot(aperture, weighted, precision=lax.Precision.HIGHEST)
    stacked = projected.reshape(-1, ZERN).T
    solved = jax.scipy.linalg.cho_solve((factor, True), stacked)
    return solved.T.reshape(leading + (2 * ZERN,))

def reference(voltages, ref_index, positions, aperture_weight):
    references = voltages[:, :, ref_index, :]
    cells = RASTER * RASTER
    blocks = TIME // TIME_DEV

    def per_channel(pair):
        volt, refs = pair

        def step(total, index):
            begin = index * TIME_DEV
            volt_blk = lax.dynamic_slice_in_dim(volt, begin, TIME_DEV, 2).astype(jnp.float32)
            ref_blk = lax.dynamic_slice_in_dim(refs, begin, TIME_DEV, 2).astype(jnp.float32)
            pos_blk = lax.dynamic_slice_in_dim(positions, begin, TIME_DEV, 0)
            real_part = ref_blk[0][:, None, :] * volt_blk[0][None] + ref_blk[1][:, None, :] * volt_blk[1][None]
            imag_part = ref_blk[0][:, None, :] * volt_blk[1][None] - ref_blk[1][:, None, :] * volt_blk[0][None]
            rows = jnp.stack([real_part, imag_part], axis=1)
            rows = jnp.moveaxis(rows, 3, 0).reshape(TIME_DEV, -1)
            return (total + jax.ops.segment_sum(rows, pos_blk, num_segments=cells), None)
        start_total = jnp.zeros((cells, REFS * 2 * STATIONS), jnp.float32)
        total, unused = lax.scan(step, start_total, jnp.arange(blocks, dtype=jnp.int32))
        return total
    sums = lax.map(per_channel, (voltages, references))
    beam = sums.reshape(CHANNELS, cells, REFS, 2, STATIONS)
    scale = (TIME / cells) ** (-0.5)
    beam = jnp.transpose(beam, (4, 0, 2, 3, 1)) * scale
    weighted, factor = fit_tables(aperture_weight)
    return finish(beam, weighted, factor, dft_real())
```

```python
import functools
import math

import jax
import jax.numpy as jnp
import numpy as np
from jax import lax
from jax.experimental import pallas as pl
from jax.experimental.pallas import tpu as pltpu
from jax.sharding import PartitionSpec as P

RASTER = 16
ZERN = 64
CELLS = RASTER * RASTER
HIGHEST = lax.Precision.HIGHEST
ROWS = (((1,), (1,)), ((), ()))


def zernike_rows():
    cell_ids = np.arange(CELLS)
    grid_x = ((cell_ids // RASTER - RASTER // 2) + 0.5) / (RASTER / 2.0)
    grid_y = ((cell_ids % RASTER - RASTER // 2) + 0.5) / (RASTER / 2.0)
    radius_sq = grid_x * grid_x + grid_y * grid_y
    in_disk = np.where(radius_sq <= 1.0, 1.0, 0.0)
    rows = []
    degree = 0
    while len(rows) < ZERN:
        for azimuth in range(-degree, degree + 1, 2):
            if len(rows) == ZERN:
                break
            order = abs(azimuth)
            power = (grid_x + 1j * grid_y) ** order
            radial = np.zeros_like(grid_x)
            for k in range((degree - order) // 2 + 1):
                weight = (
                    (-1) ** k
                    * math.factorial(degree - k)
                    / (
                        math.factorial(k)
                        * math.factorial((degree + order) // 2 - k)
                        * math.factorial((degree - order) // 2 - k)
                    )
                )
                radial = radial + weight * radius_sq ** ((degree - 2 * k - order) // 2)
            if azimuth > 0:
                row = radial * power.real * math.sqrt(2.0 * (degree + 1))
            elif azimuth < 0:
                row = radial * power.imag * math.sqrt(2.0 * (degree + 1))
            else:
                row = radial * math.sqrt(degree + 1.0)
            rows.append(row * in_disk)
        degree += 1
    return np.stack(rows).astype(np.float32)


def dft_rows():
    cell_ids = np.arange(CELLS)
    a = cell_ids // RASTER - RASTER // 2
    b = cell_ids % RASTER - RASTER // 2
    phases = (a[:, None] * a[None, :] + b[:, None] * b[None, :]) % RASTER
    angles = phases * (2.0 * math.pi / RASTER)
    return np.concatenate([np.cos(angles), -np.sin(angles)], axis=1).astype(np.float32)


def pick_kernel(index_ref, volt_ref, out_ref):
    stations = volt_ref.shape[2]
    refs = out_ref.shape[2]
    first = lax.axis_index("stat") * stations
    row = lax.broadcasted_iota(jnp.int32, (refs, stations), 0)
    lane = lax.broadcasted_iota(jnp.int32, (refs, stations), 1)
    wanted = jnp.zeros((refs, stations), jnp.int32)
    for r in range(refs):
        wanted = jnp.where(row == r, index_ref[r] - first, wanted)
    select = jnp.where(lane == wanted, 1.0, 0.0).astype(jnp.bfloat16)
    out_ref[0, 0] = jnp.dot(
        select, volt_ref[0, 0], preferred_element_type=jnp.float32
    ).astype(jnp.bfloat16)


def pick(ref_index, voltages):
    chans, parts, stations, times = voltages.shape
    refs = ref_index.shape[0]
    return pl.pallas_call(
        pick_kernel,
        grid=(chans, parts),
        in_specs=[
            pl.BlockSpec(memory_space=pltpu.SMEM),
            pl.BlockSpec((1, 1, stations, times), lambda c, k: (c, k, 0, 0)),
        ],
        out_specs=pl.BlockSpec((1, 1, refs, times), lambda c, k: (c, k, 0, 0)),
        out_shape=jax.ShapeDtypeStruct((chans, parts, refs, times), jnp.bfloat16),
        name="pick_references",
    )(ref_index, voltages)


def invert(gram):
    size = gram.shape[0]
    row = lax.broadcasted_iota(jnp.int32, (size, size), 0)
    lane = lax.broadcasted_iota(jnp.int32, (size, size), 1)
    work = jnp.concatenate([gram, jnp.where(row == lane, 1.0, 0.0)], axis=1)
    row = lax.broadcasted_iota(jnp.int32, work.shape, 0)
    for k in range(size):
        pivot = work[k : k + 1, :] / work[k : k + 1, k : k + 1]
        work = jnp.where(row == k, pivot, work - work[:, k : k + 1] * pivot)
    return work[:, size:]


def split(value, parts):
    pieces = []
    for _ in range(parts):
        piece = value.astype(jnp.bfloat16)
        pieces.append(piece)
        value = value - piece.astype(jnp.float32)
    return pieces


def tables_kernel(scale, weight_ref, zern_ref, dft_ref, pos_ref, out_ref):
    zern = zern_ref[...]
    weighted = zern * weight_ref[...]
    gram = lax.dot_general(weighted, zern, ROWS, precision=HIGHEST, preferred_element_type=jnp.float32)
    field = jnp.dot(weighted, dft_ref[...], precision=HIGHEST, preferred_element_type=jnp.float32)
    fit = jnp.dot(invert(gram), field, precision=HIGHEST, preferred_element_type=jnp.float32) * scale
    fit = jnp.concatenate([fit[:, :CELLS], fit[:, CELLS:]], axis=0)
    pieces = split(fit, 3)
    times = pos_ref.shape[1]
    step = 512
    cell = lax.broadcasted_iota(jnp.int32, (CELLS, step), 0)
    for begin in range(0, times, step):
        onehot = jnp.where(cell == pos_ref[:, begin : begin + step], 1.0, 0.0).astype(jnp.bfloat16)
        total = jnp.dot(pieces[0], onehot, preferred_element_type=jnp.float32)
        for piece in pieces[1:]:
            total = total + jnp.dot(piece, onehot, preferred_element_type=jnp.float32)
        out_ref[:, begin : begin + step] = total


def tables(weight, positions, scale):
    times = positions.shape[0]
    return pl.pallas_call(
        functools.partial(tables_kernel, scale),
        out_shape=jax.ShapeDtypeStruct((2 * ZERN, times), jnp.float32),
        name="fit_tables",
        cost_estimate=pl.CostEstimate(flops=4_000_000_000, bytes_accessed=2_000_000, transcendentals=0),
    )(weight.reshape(1, CELLS), jnp.asarray(zernike_rows()), jnp.asarray(dft_rows()), positions.reshape(1, times))


STEP = 512


def correlate_kernel(volt_ref, *rest):
    ref_parts = rest[:-6]
    table_ref, out_ref, refs_ref, left_a, left_b, total_ref = rest[-6:]
    chans, parts, stations, times = volt_ref.shape
    refs = refs_ref.shape[2]
    steps = times // STEP
    picked = ref_parts[0][...]
    for other in ref_parts[1:]:
        picked = picked + other[...]
    refs_ref[...] = picked.astype(jnp.float32)

    def produce(chan, step, left_ref):
        span = pl.ds(step * STEP, STEP)
        for r in range(refs):
            real = refs_ref[chan, 0, r : r + 1, span]
            imag = refs_ref[chan, 1, r : r + 1, span]
            for half in range(0, ZERN, 16):
                table_r = table_ref[half : half + 16, span]
                table_i = table_ref[ZERN + half : ZERN + half + 16, span]
                for at, value in (
                    (half, real * table_r + imag * table_i),
                    (ZERN + half, real * table_i - imag * table_r),
                ):
                    high, low = split(value, 2)
                    rows = pl.ds(r * 2 * ZERN + at, 16)
                    left_ref[rows, 0:STEP] = high
                    left_ref[rows, STEP : 2 * STEP] = low

    def consume(chan, step, left_ref):
        span = pl.ds(step * STEP, STEP)
        right = volt_ref[chan, :, :, span].reshape(parts * stations, STEP)
        right = jnp.concatenate([right, right], axis=1)
        product = lax.dot_general(left_ref[...], right, ROWS, preferred_element_type=jnp.float32)
        if step == 0:
            total_ref[...] = product
        else:
            total_ref[...] += product

    def finish(chan):
        for r in range(refs):
            top = total_ref[r * 2 * ZERN : r * 2 * ZERN + ZERN, :]
            low = total_ref[r * 2 * ZERN + ZERN : (r + 1) * 2 * ZERN, :]
            real = top[:, :stations] - low[:, stations:]
            imag = top[:, stations:] + low[:, :stations]
            both = jnp.concatenate([real, imag], axis=0).T
            out_ref[chan, pl.ds(r, stations, stride=refs), :] = both

    order = [(chan, step) for chan in range(chans) for step in range(steps)]
    buffers = (left_a, left_b)
    produce(*order[0], buffers[0])
    for i, (chan, step) in enumerate(order):
        if i + 1 < len(order):
            produce(*order[i + 1], buffers[(i + 1) % 2])
        consume(chan, step, buffers[i % 2])
        if step == steps - 1:
            finish(chan)


def correlate(voltages, ref_parts, table):
    chans, parts, stations, times = voltages.shape
    refs = ref_parts[0].shape[2]
    vmem = pl.BlockSpec(memory_space=pltpu.VMEM)
    return pl.pallas_call(
        correlate_kernel,
        in_specs=[vmem] * (2 + len(ref_parts)),
        out_specs=vmem,
        out_shape=jax.ShapeDtypeStruct((chans, stations * refs, 2 * ZERN), jnp.float32),
        scratch_shapes=[
            pltpu.VMEM((chans, parts, refs, times), jnp.float32),
            pltpu.VMEM((refs * 2 * ZERN, 2 * STEP), jnp.bfloat16),
            pltpu.VMEM((refs * 2 * ZERN, 2 * STEP), jnp.bfloat16),
            pltpu.VMEM((refs * 2 * ZERN, parts * stations), jnp.float32),
        ],
        compiler_params=pltpu.CompilerParams(vmem_limit_bytes=40 * 2**20),
        cost_estimate=pl.CostEstimate(flops=8_600_000_000, bytes_accessed=5_000_000, transcendentals=0),
        name="correlate",
    )(voltages, *ref_parts, table)


def collect_kernel(*refs):
    *ins, out_ref = refs
    chan = lax.axis_index("chan")
    chan_count = lax.axis_size("chan")
    tm_count = len(ins) // chan_count
    for dc in range(chan_count):
        total = ins[dc][...]
        for dt in range(1, tm_count):
            total = total + ins[dt * chan_count + dc][...]
        source = jnp.bitwise_xor(chan, dc)
        for c in range(total.shape[0]):
            out_ref[:, source * total.shape[0] + c] = total[c]


def collect(pieces, chan_count):
    chans, stations, refs, terms = pieces[0].shape
    vmem = pl.BlockSpec(memory_space=pltpu.VMEM)
    return pl.pallas_call(
        collect_kernel,
        in_specs=[vmem] * len(pieces),
        out_specs=vmem,
        out_shape=jax.ShapeDtypeStruct((stations, chans * chan_count, refs, terms), jnp.float32),
        name="sum_time_blocks",
    )(*pieces)


def on_device(voltages, ref_index, positions, aperture_weight):
    chans, parts, stations, times = voltages.shape
    refs = ref_index.shape[0]
    stat_count = lax.axis_size("stat")
    tm_count = lax.axis_size("tm")
    chan_count = lax.axis_size("chan")
    picked = pick(ref_index, voltages)
    ref_parts = [picked]
    for shift in range(1, stat_count):
        ref_parts.append(
            lax.ppermute(picked, "stat", [(i, (i + shift) % stat_count) for i in range(stat_count)])
        )
    scale = (tm_count * times / CELLS) ** (-0.5)
    table = tables(aperture_weight, positions, scale)
    sums = correlate(voltages, ref_parts, table)
    owners = tm_count * chan_count
    sums = sums.reshape(chans, owners, stations // owners, refs, 2 * ZERN)
    chan = lax.axis_index("chan")
    tm = lax.axis_index("tm")
    pieces = []
    for dt in range(tm_count):
        for dc in range(chan_count):
            owner = (tm ^ dt) * chan_count + (chan ^ dc)
            block = lax.dynamic_index_in_dim(sums, owner, 1, keepdims=False)
            if dt or dc:
                pairs = [
                    (c * tm_count + t, (c ^ dc) * tm_count + (t ^ dt))
                    for c in range(chan_count)
                    for t in range(tm_count)
                ]
                block = lax.ppermute(block, ("chan", "tm"), pairs)
            pieces.append(block)
    return collect(pieces, chan_count)


def solution(mesh):
    in_specs = (P("chan", None, "stat", "tm"), P(), P("tm"), P())
    out_specs = P(("stat", "tm", "chan"), None, None, None)
    return jax.shard_map(
        on_device, mesh=mesh, in_specs=in_specs, out_specs=out_specs, check_vma=False
    )
```

```python
import functools
import math

import jax
import jax.numpy as jnp
import numpy as np
from jax import lax
from jax.experimental import pallas as pl
from jax.experimental.pallas import tpu as pltpu
from jax.sharding import PartitionSpec as P

RASTER = 16
ZERN = 64
CELLS = RASTER * RASTER
HIGHEST = lax.Precision.HIGHEST
ROWS = (((1,), (1,)), ((), ()))
GROUP = 16
STEP = 512


def zernike_rows():
    cell_ids = np.arange(CELLS)
    grid_x = ((cell_ids // RASTER - RASTER // 2) + 0.5) / (RASTER / 2.0)
    grid_y = ((cell_ids % RASTER - RASTER // 2) + 0.5) / (RASTER / 2.0)
    radius_sq = grid_x * grid_x + grid_y * grid_y
    in_disk = np.where(radius_sq <= 1.0, 1.0, 0.0)
    rows = []
    degree = 0
    while len(rows) < ZERN:
        for azimuth in range(-degree, degree + 1, 2):
            if len(rows) == ZERN:
                break
            order = abs(azimuth)
            power = (grid_x + 1j * grid_y) ** order
            radial = np.zeros_like(grid_x)
            for k in range((degree - order) // 2 + 1):
                weight = (
                    (-1) ** k
                    * math.factorial(degree - k)
                    / (
                        math.factorial(k)
                        * math.factorial((degree + order) // 2 - k)
                        * math.factorial((degree - order) // 2 - k)
                    )
                )
                radial = radial + weight * radius_sq ** ((degree - 2 * k - order) // 2)
            if azimuth > 0:
                row = radial * power.real * math.sqrt(2.0 * (degree + 1))
            elif azimuth < 0:
                row = radial * power.imag * math.sqrt(2.0 * (degree + 1))
            else:
                row = radial * math.sqrt(degree + 1.0)
            rows.append(row * in_disk)
        degree += 1
    return np.stack(rows).astype(np.float32)


def dft_rows():
    cell_ids = np.arange(CELLS)
    a = cell_ids // RASTER - RASTER // 2
    b = cell_ids % RASTER - RASTER // 2
    phases = (a[:, None] * a[None, :] + b[:, None] * b[None, :]) % RASTER
    angles = phases * (2.0 * math.pi / RASTER)
    return np.concatenate([np.cos(angles), -np.sin(angles)], axis=1).astype(np.float32)


def pick_kernel(index_ref, volt_ref, out_ref, rows_ref):
    chans, parts, stations, _ = volt_ref.shape
    refs = out_ref.shape[2]
    first = lax.axis_index("stat") * stations
    rows_ref[...] = jnp.zeros_like(rows_ref)
    for r in range(refs):
        local = index_ref[r] - first

        @pl.when(jnp.logical_and(local >= 0, local < stations))
        def _():
            begin = pl.multiple_of(local // GROUP * GROUP, GROUP)
            for c in range(chans):
                for k in range(parts):
                    group = volt_ref[c, k, pl.ds(begin, GROUP), :].astype(jnp.float32)
                    row = lax.broadcasted_iota(jnp.int32, group.shape, 0)
                    group = jnp.where(row == local - begin, group, 0.0)
                    rows_ref[c, k, r : r + 1, :] = jnp.sum(group, axis=0, keepdims=True)

    out_ref[...] = rows_ref[...].astype(jnp.bfloat16)


def pick(ref_index, voltages):
    chans, parts, _, times = voltages.shape
    refs = ref_index.shape[0]
    vmem = pl.BlockSpec(memory_space=pltpu.VMEM)
    return pl.pallas_call(
        pick_kernel,
        in_specs=[pl.BlockSpec(memory_space=pltpu.SMEM), vmem],
        out_specs=vmem,
        out_shape=jax.ShapeDtypeStruct((chans, parts, refs, times), jnp.bfloat16),
        scratch_shapes=[pltpu.VMEM((chans, parts, refs, times), jnp.float32)],
        compiler_params=pltpu.CompilerParams(vmem_limit_bytes=8 * 2**20),
        name="pick_references",
    )(ref_index, voltages)


def invert(gram):
    size = gram.shape[0]
    row = lax.broadcasted_iota(jnp.int32, (size, size), 0)
    lane = lax.broadcasted_iota(jnp.int32, (size, size), 1)
    work = jnp.concatenate([gram, jnp.where(row == lane, 1.0, 0.0)], axis=1)
    row = lax.broadcasted_iota(jnp.int32, work.shape, 0)
    for k in range(size):
        pivot = work[k : k + 1, :] / work[k : k + 1, k : k + 1]
        work = jnp.where(row == k, pivot, work - work[:, k : k + 1] * pivot)
    return work[:, size:]


def split(value, parts):
    pieces = []
    for _ in range(parts):
        piece = value.astype(jnp.bfloat16)
        pieces.append(piece)
        value = value - piece.astype(jnp.float32)
    return pieces


def tables_kernel(scale, weight_ref, zern_ref, dft_ref, pos_ref, out_ref):
    weighted = zern_ref[...] * (weight_ref[...] * scale)
    field = jnp.dot(weighted, dft_ref[...], precision=HIGHEST, preferred_element_type=jnp.float32)
    field = jnp.concatenate([field[:, :CELLS], field[:, CELLS:]], axis=0)
    pieces = split(field, 3)
    times = pos_ref.shape[1]
    cell = lax.broadcasted_iota(jnp.int32, (CELLS, STEP), 0)
    for begin in range(0, times, STEP):
        onehot = jnp.where(cell == pos_ref[:, begin : begin + STEP], 1.0, 0.0).astype(jnp.bfloat16)
        total = jnp.dot(pieces[0], onehot, preferred_element_type=jnp.float32)
        for piece in pieces[1:]:
            total = total + jnp.dot(piece, onehot, preferred_element_type=jnp.float32)
        out_ref[:, begin : begin + STEP] = total


def tables(weight, positions, scale):
    times = positions.shape[0]
    return pl.pallas_call(
        functools.partial(tables_kernel, scale),
        out_shape=jax.ShapeDtypeStruct((2 * ZERN, times), jnp.float32),
        name="projection_per_sample",
        compiler_params=pltpu.CompilerParams(vmem_limit_bytes=12 * 2**20),
        cost_estimate=pl.CostEstimate(flops=4_000_000_000, bytes_accessed=2_000_000, transcendentals=0),
    )(weight.reshape(1, CELLS), jnp.asarray(zernike_rows()), jnp.asarray(dft_rows()), positions.reshape(1, times))


def inverse_kernel(weight_ref, zern_ref, out_ref):
    zern = zern_ref[...]
    gram = lax.dot_general(
        zern * weight_ref[...], zern, ROWS, precision=HIGHEST, preferred_element_type=jnp.float32
    )
    inverse = invert(gram)
    zeros = jnp.zeros_like(inverse)
    out_ref[...] = jnp.concatenate(
        [jnp.concatenate([inverse, zeros], axis=1), jnp.concatenate([zeros, inverse], axis=1)], axis=0
    )


def gram_inverse(weight):
    return pl.pallas_call(
        inverse_kernel,
        out_shape=jax.ShapeDtypeStruct((2 * ZERN, 2 * ZERN), jnp.float32),
        name="gram_inverse",
        compiler_params=pltpu.CompilerParams(vmem_limit_bytes=4 * 2**20),
        cost_estimate=pl.CostEstimate(flops=5_000_000_000, bytes_accessed=200_000, transcendentals=0),
    )(weight.reshape(1, CELLS), jnp.asarray(zernike_rows()))


def correlate_kernel(owners, volt_ref, *rest):
    table_ref, *out_refs, refs_ref, left_a, left_b, total_ref = rest[-(5 + (len(owners) if owners else 1)) :]
    ref_parts = rest[: len(rest) - (5 + len(out_refs))]
    chans, parts, stations, times = volt_ref.shape
    refs = refs_ref.shape[2]
    steps = times // STEP
    picked = ref_parts[0][...]
    for other in ref_parts[1:]:
        picked = picked + other[...]
    refs_ref[...] = picked.astype(jnp.float32)
    own = stations // len(out_refs)
    begins = [0]
    if owners:
        tm, chan_at, chan_count = lax.axis_index("tm"), lax.axis_index("chan"), lax.axis_size("chan")
        begins = [
            pl.multiple_of(
                (jnp.bitwise_xor(tm, dt) * chan_count + jnp.bitwise_xor(chan_at, dc)) * own, own
            )
            for dt, dc in owners
        ]

    def produce(chan, step, left_ref):
        span = pl.ds(step * STEP, STEP)
        for r in range(refs):
            real = refs_ref[chan, 0, r : r + 1, span]
            imag = refs_ref[chan, 1, r : r + 1, span]
            for half in range(0, ZERN, 16):
                table_r = table_ref[half : half + 16, span]
                table_i = table_ref[ZERN + half : ZERN + half + 16, span]
                for at, value in (
                    (half, real * table_r + imag * table_i),
                    (ZERN + half, real * table_i - imag * table_r),
                ):
                    high, low = split(value, 2)
                    rows = pl.ds(r * 2 * ZERN + at, 16)
                    left_ref[rows, 0:STEP] = high
                    left_ref[rows, STEP : 2 * STEP] = low

    def consume(chan, step, left_ref):
        span = pl.ds(step * STEP, STEP)
        right = jnp.concatenate(
            [volt_ref[chan, k, pl.ds(begin, own), span] for k in range(parts) for begin in begins], axis=0
        )
        right = jnp.concatenate([right, right], axis=1)
        product = lax.dot_general(left_ref[...], right, ROWS, preferred_element_type=jnp.float32)
        if step == 0:
            total_ref[...] = product
        else:
            total_ref[...] += product

    def finish(chan):
        for r in range(refs):
            top = total_ref[r * 2 * ZERN : r * 2 * ZERN + ZERN, :]
            low = total_ref[r * 2 * ZERN + ZERN : (r + 1) * 2 * ZERN, :]
            real = top[:, :stations] - low[:, stations:]
            imag = top[:, stations:] + low[:, :stations]
            both = jnp.concatenate([real, imag], axis=0).T
            for i, out_ref in enumerate(out_refs):
                out_ref[chan, pl.ds(r, own, stride=refs), :] = both[i * own : (i + 1) * own]

    order = [(chan, step) for chan in range(chans) for step in range(steps)]
    buffers = (left_a, left_b)
    produce(*order[0], buffers[0])
    for i, (chan, step) in enumerate(order):
        if i + 1 < len(order):
            produce(*order[i + 1], buffers[(i + 1) % 2])
        consume(chan, step, buffers[i % 2])
        if step == steps - 1:
            finish(chan)


def correlate(voltages, ref_parts, table, owners):
    chans, parts, stations, times = voltages.shape
    refs = ref_parts[0].shape[2]
    vmem = pl.BlockSpec(memory_space=pltpu.VMEM)
    blocks = len(owners) if owners else 1
    return pl.pallas_call(
        functools.partial(correlate_kernel, owners),
        in_specs=[vmem] * (2 + len(ref_parts)),
        out_specs=[vmem] * blocks,
        out_shape=[jax.ShapeDtypeStruct((chans, stations // blocks * refs, 2 * ZERN), jnp.float32)] * blocks,
        scratch_shapes=[
            pltpu.VMEM((chans, parts, refs, times), jnp.float32),
            pltpu.VMEM((refs * 2 * ZERN, 2 * STEP), jnp.bfloat16),
            pltpu.VMEM((refs * 2 * ZERN, 2 * STEP), jnp.bfloat16),
            pltpu.VMEM((refs * 2 * ZERN, parts * stations), jnp.float32),
        ],
        compiler_params=pltpu.CompilerParams(vmem_limit_bytes=24 * 2**20),
        cost_estimate=pl.CostEstimate(flops=8_600_000_000, bytes_accessed=5_000_000, transcendentals=0),
        name="correlate",
    )(voltages, *ref_parts, table)


def collect_kernel(*refs):
    *ins, inverse_ref, out_ref = refs
    chan = lax.axis_index("chan")
    chan_count = lax.axis_size("chan")
    tm_count = len(ins) // chan_count
    chans, stations, rows, terms = ins[0].shape
    for dc in range(chan_count):
        total = ins[dc][...]
        for dt in range(1, tm_count):
            total = total + ins[dt * chan_count + dc][...]
        solved = jnp.dot(
            total.reshape(chans * stations * rows, terms),
            inverse_ref[...],
            precision=HIGHEST,
            preferred_element_type=jnp.float32,
        ).reshape(total.shape)
        source = jnp.bitwise_xor(chan, dc)
        for c in range(chans):
            out_ref[:, source * chans + c] = solved[c]


def collect(pieces, inverse, chan_count):
    chans, stations, refs, terms = pieces[0].shape
    vmem = pl.BlockSpec(memory_space=pltpu.VMEM)
    return pl.pallas_call(
        collect_kernel,
        in_specs=[vmem] * (len(pieces) + 1),
        out_specs=vmem,
        out_shape=jax.ShapeDtypeStruct((stations, chans * chan_count, refs, terms), jnp.float32),
        compiler_params=pltpu.CompilerParams(vmem_limit_bytes=8 * 2**20),
        name="sum_and_solve",
    )(*pieces, inverse)


def on_device(voltages, ref_index, positions, aperture_weight):
    chans, parts, stations, times = voltages.shape
    refs = ref_index.shape[0]
    stat_count = lax.axis_size("stat")
    tm_count = lax.axis_size("tm")
    chan_count = lax.axis_size("chan")
    picked = pick(ref_index, voltages)
    ref_parts = [picked]
    for shift in range(1, stat_count):
        ref_parts.append(
            lax.ppermute(picked, "stat", [(i, (i + shift) % stat_count) for i in range(stat_count)])
        )
    scale = (tm_count * times / CELLS) ** (-0.5)
    table = tables(aperture_weight, positions, scale)
    inverse = gram_inverse(aperture_weight)
    owners = [(dt, dc) for dt in range(tm_count) for dc in range(chan_count)]
    own = stations // len(owners)
    block = (chans, own, refs, 2 * ZERN)
    if own % GROUP == 0:
        sums = [x.reshape(block) for x in correlate(voltages, ref_parts, table, owners)]
    else:
        whole = correlate(voltages, ref_parts, table, None)[0].reshape((chans, len(owners)) + block[1:])
        tm, chan = lax.axis_index("tm"), lax.axis_index("chan")
        sums = [
            lax.dynamic_index_in_dim(whole, (tm ^ dt) * chan_count + (chan ^ dc), 1, keepdims=False)
            for dt, dc in owners
        ]
    pieces = []
    for (dt, dc), x in zip(owners, sums):
        if dt or dc:
            pairs = [
                (c * tm_count + t, (c ^ dc) * tm_count + (t ^ dt))
                for c in range(chan_count)
                for t in range(tm_count)
            ]
            x = lax.ppermute(x, ("chan", "tm"), pairs)
        pieces.append(x)
    return collect(pieces, inverse, chan_count)


def solution(mesh):
    in_specs = (P("chan", None, "stat", "tm"), P(), P("tm"), P())
    out_specs = P(("stat", "tm", "chan"), None, None, None)
    return jax.shard_map(
        on_device, mesh=mesh, in_specs=in_specs, out_specs=out_specs, check_vma=False
    )
```

```python
import functools
import math

import jax
import jax.numpy as jnp
import numpy as np
from jax import lax
from jax.experimental import pallas as pl
from jax.experimental.pallas import tpu as pltpu
from jax.sharding import PartitionSpec as P

RASTER = 16
ZERN = 64
CELLS = RASTER * RASTER
HIGHEST = lax.Precision.HIGHEST
ROWS = (((1,), (1,)), ((), ()))
GROUP = 16
STEP = 512
LEVELS = 64.0
MOST = 32500.0


def zernike_rows():
    cell_ids = np.arange(CELLS)
    grid_x = ((cell_ids // RASTER - RASTER // 2) + 0.5) / (RASTER / 2.0)
    grid_y = ((cell_ids % RASTER - RASTER // 2) + 0.5) / (RASTER / 2.0)
    radius_sq = grid_x * grid_x + grid_y * grid_y
    in_disk = np.where(radius_sq <= 1.0, 1.0, 0.0)
    rows = []
    degree = 0
    while len(rows) < ZERN:
        for azimuth in range(-degree, degree + 1, 2):
            if len(rows) == ZERN:
                break
            order = abs(azimuth)
            power = (grid_x + 1j * grid_y) ** order
            radial = np.zeros_like(grid_x)
            for k in range((degree - order) // 2 + 1):
                weight = (
                    (-1) ** k
                    * math.factorial(degree - k)
                    / (
                        math.factorial(k)
                        * math.factorial((degree + order) // 2 - k)
                        * math.factorial((degree - order) // 2 - k)
                    )
                )
                radial = radial + weight * radius_sq ** ((degree - 2 * k - order) // 2)
            if azimuth > 0:
                row = radial * power.real * math.sqrt(2.0 * (degree + 1))
            elif azimuth < 0:
                row = radial * power.imag * math.sqrt(2.0 * (degree + 1))
            else:
                row = radial * math.sqrt(degree + 1.0)
            rows.append(row * in_disk)
        degree += 1
    return np.stack(rows).astype(np.float32)


def dft_rows():
    cell_ids = np.arange(CELLS)
    a = cell_ids // RASTER - RASTER // 2
    b = cell_ids % RASTER - RASTER // 2
    phases = (a[:, None] * a[None, :] + b[:, None] * b[None, :]) % RASTER
    angles = phases * (2.0 * math.pi / RASTER)
    return np.concatenate([np.cos(angles), -np.sin(angles)], axis=1).astype(np.float32)


def pick_kernel(index_ref, volt_ref, *rest):
    *out_refs, group_ref, rows_ref, sems = rest
    chans, parts, stations, _ = volt_ref.shape
    refs = rows_ref.shape[2]
    first = lax.axis_index("stat") * stations

    def each_owned(work):
        for r in range(refs):
            local = index_ref[r] - first
            pl.when(jnp.logical_and(local >= 0, local < stations))(functools.partial(work, r, local))

    def copy(r, local):
        begin = pl.multiple_of(local // GROUP * GROUP, GROUP)
        return pltpu.make_async_copy(volt_ref.at[:, :, pl.ds(begin, GROUP), :], group_ref.at[r], sems.at[r])

    def fill(r, local):
        copy(r, local).wait()
        for c in range(chans):
            for k in range(parts):
                group = group_ref[r, c, k].astype(jnp.float32)
                row = lax.broadcasted_iota(jnp.int32, group.shape, 0)
                group = jnp.where(row == lax.rem(local, GROUP), group, 0.0)
                rows_ref[c, k, r : r + 1, :] = jnp.sum(group, axis=0, keepdims=True)

    each_owned(lambda r, local: copy(r, local).start())
    rows_ref[...] = jnp.zeros_like(rows_ref)
    each_owned(fill)
    for c, out_ref in enumerate(out_refs):
        out_ref[...] = rows_ref[c].astype(jnp.bfloat16)


def pick(ref_index, voltages):
    chans, parts, _, times = voltages.shape
    refs = ref_index.shape[0]
    vmem = pl.BlockSpec(memory_space=pltpu.VMEM)
    return pl.pallas_call(
        pick_kernel,
        in_specs=[pl.BlockSpec(memory_space=pltpu.SMEM), pl.BlockSpec(memory_space=pl.ANY)],
        out_specs=[vmem] * chans,
        out_shape=[jax.ShapeDtypeStruct((parts, refs, times), jnp.bfloat16)] * chans,
        scratch_shapes=[
            pltpu.VMEM((refs, chans, parts, GROUP, times), jnp.bfloat16),
            pltpu.VMEM((chans, parts, refs, times), jnp.float32),
            pltpu.SemaphoreType.DMA((refs,)),
        ],
        compiler_params=pltpu.CompilerParams(vmem_limit_bytes=8 * 2**20),
        name="pick_references",
    )(ref_index, voltages)


def invert(gram):
    size = gram.shape[0]
    row = lax.broadcasted_iota(jnp.int32, (size, size), 0)
    lane = lax.broadcasted_iota(jnp.int32, (size, size), 1)
    work = jnp.concatenate([gram, jnp.where(row == lane, 1.0, 0.0)], axis=1)
    row = lax.broadcasted_iota(jnp.int32, work.shape, 0)
    for k in range(size):
        pivot = work[k : k + 1, :] / work[k : k + 1, k : k + 1]
        work = jnp.where(row == k, pivot, work - work[:, k : k + 1] * pivot)
    return work[:, size:]


def split(value, parts):
    pieces = []
    for _ in range(parts):
        piece = value.astype(jnp.bfloat16)
        pieces.append(piece)
        value = value - piece.astype(jnp.float32)
    return pieces


def tables_kernel(scale, weight_ref, zern_ref, dft_ref, pos_ref, out_ref):
    weighted = zern_ref[...] * (weight_ref[...] * scale)
    field = jnp.dot(weighted, dft_ref[...], precision=HIGHEST, preferred_element_type=jnp.float32)
    field = jnp.concatenate([field[:, :CELLS], field[:, CELLS:]], axis=0)
    pieces = split(field, 3)
    times = pos_ref.shape[1]
    cell = lax.broadcasted_iota(jnp.int32, (CELLS, STEP), 0)
    for begin in range(0, times, STEP):
        onehot = jnp.where(cell == pos_ref[:, begin : begin + STEP], 1.0, 0.0).astype(jnp.bfloat16)
        total = jnp.dot(pieces[0], onehot, preferred_element_type=jnp.float32)
        for piece in pieces[1:]:
            total = total + jnp.dot(piece, onehot, preferred_element_type=jnp.float32)
        out_ref[:, begin : begin + STEP] = total


def tables(weight, positions, scale):
    times = positions.shape[0]
    return pl.pallas_call(
        functools.partial(tables_kernel, scale),
        out_shape=jax.ShapeDtypeStruct((2 * ZERN, times), jnp.float32),
        name="projection_per_sample",
        compiler_params=pltpu.CompilerParams(vmem_limit_bytes=12 * 2**20),
        cost_estimate=pl.CostEstimate(flops=4_000_000_000, bytes_accessed=2_000_000, transcendentals=0),
    )(weight.reshape(1, CELLS), jnp.asarray(zernike_rows()), jnp.asarray(dft_rows()), positions.reshape(1, times))


def inverse_kernel(weight_ref, zern_ref, out_ref):
    zern = zern_ref[...]
    gram = lax.dot_general(
        zern * weight_ref[...], zern, ROWS, precision=HIGHEST, preferred_element_type=jnp.float32
    )
    inverse = invert(gram)
    zeros = jnp.zeros_like(inverse)
    out_ref[...] = jnp.concatenate(
        [jnp.concatenate([inverse, zeros], axis=1), jnp.concatenate([zeros, inverse], axis=1)], axis=0
    )


def gram_inverse(weight):
    return pl.pallas_call(
        inverse_kernel,
        out_shape=jax.ShapeDtypeStruct((2 * ZERN, 2 * ZERN), jnp.float32),
        name="gram_inverse",
        compiler_params=pltpu.CompilerParams(vmem_limit_bytes=4 * 2**20),
        cost_estimate=pl.CostEstimate(flops=5_000_000_000, bytes_accessed=200_000, transcendentals=0),
    )(weight.reshape(1, CELLS), jnp.asarray(zernike_rows()))


def correlate_kernel(chan, owners, last, *args):
    (volt_ref, first_ref, second_ref, table_ref), args = args[:4], args[4:]
    before_refs, args = args[: 3 * last], args[3 * last :]
    out_refs, (refs_ref, left_a, left_b, total_ref, stage_ref) = args[:-5], args[-5:]
    _, parts, stations, times = volt_ref.shape
    refs = refs_ref.shape[1]
    steps = times // STEP
    refs_ref[...] = (first_ref[...] + second_ref[...]).astype(jnp.float32)
    own = stations // (len(owners) if owners else 1)
    begins = [0]
    if owners:
        tm, chan_at, chan_count = lax.axis_index("tm"), lax.axis_index("chan"), lax.axis_size("chan")
        begins = [
            pl.multiple_of(
                (jnp.bitwise_xor(tm, dt) * chan_count + jnp.bitwise_xor(chan_at, dc)) * own, own
            )
            for dt, dc in owners
        ]

    def produce(step, left_ref):
        span = pl.ds(step * STEP, STEP)
        for r in range(refs):
            real = refs_ref[0, r : r + 1, span]
            imag = refs_ref[1, r : r + 1, span]
            for half in range(0, ZERN, 16):
                table_r = table_ref[half : half + 16, span]
                table_i = table_ref[ZERN + half : ZERN + half + 16, span]
                for at, value in (
                    (half, real * table_r + imag * table_i),
                    (ZERN + half, real * table_i - imag * table_r),
                ):
                    high, low = split(value, 2)
                    rows = pl.ds(r * 2 * ZERN + at, 16)
                    left_ref[rows, 0:STEP] = high
                    left_ref[rows, STEP : 2 * STEP] = low

    def consume(step, left_ref):
        span = pl.ds(step * STEP, STEP)
        right = jnp.concatenate(
            [volt_ref[chan, k, pl.ds(begin, own), span] for k in range(parts) for begin in begins], axis=0
        )
        right = jnp.concatenate([right, right], axis=1)
        product = lax.dot_general(left_ref[...], right, ROWS, preferred_element_type=jnp.float32)
        if step == 0:
            total_ref[...] = product
        else:
            total_ref[...] += product

    buffers = (left_a, left_b)
    produce(0, buffers[0])
    for step in range(steps):
        if step + 1 < steps:
            produce(step + 1, buffers[(step + 1) % 2])
        consume(step, buffers[step % 2])
    kept = lax.broadcasted_iota(jnp.int32, (1, stations), 1) < own
    levels = []
    for r in range(refs):
        top = total_ref[r * 2 * ZERN : r * 2 * ZERN + ZERN, :]
        low = total_ref[r * 2 * ZERN + ZERN : (r + 1) * 2 * ZERN, :]
        real = top[:, :stations] - low[:, stations:]
        imag = top[:, stations:] + low[:, :stations]
        both = jnp.concatenate([real, imag], axis=0)
        if owners:
            most = jnp.maximum(jnp.max(jnp.abs(both), axis=0, keepdims=True), 1e-30)
            level = jnp.floor(jnp.log2(most) * LEVELS) + 1.0
            levels.append(level)
            rounded = jnp.floor(both * (jnp.exp2(level * (-1.0 / LEVELS)) * MOST) + 0.5)
            both = jnp.where(kept, both, rounded)
        stage_ref[pl.ds(r, stations, stride=refs), :] = both.T
    if not owners:
        out_refs[0][...] = stage_ref[...]
        return
    rows = own * refs
    level = jnp.concatenate(levels, axis=0)
    sent = stage_ref[rows:, :].astype(jnp.int32).astype(jnp.int16)
    if not last:
        out_refs[0][...] = stage_ref[:rows, :]
        out_refs[1][...] = sent
        out_refs[2][...] = level
        return
    out_refs[0][0] = before_refs[0][...]
    out_refs[0][1] = stage_ref[:rows, :]
    levels = jnp.concatenate([before_refs[2][...], level], axis=0).astype(jnp.int32).astype(jnp.int16)
    for i, out_ref in enumerate(out_refs[1:]):
        out_ref[:rows, :] = before_refs[1][i * rows : (i + 1) * rows, :]
        out_ref[rows : 2 * rows, :] = sent[i * rows : (i + 1) * rows]
        out_ref[2 * rows :, :] = levels


def correlate(voltages, ref_parts, table, owners):
    chans, parts, stations, times = voltages.shape
    refs = ref_parts[0][0].shape[1]
    vmem = pl.BlockSpec(memory_space=pltpu.VMEM)
    rows = stations // (len(owners) if owners else 1) * refs
    plain = jax.ShapeDtypeStruct((stations * refs, 2 * ZERN), jnp.float32)
    sums = []
    for chan in range(chans):
        last = owners is not None and chan == chans - 1
        if last:
            shapes = [jax.ShapeDtypeStruct((chans, rows, 2 * ZERN), jnp.float32)]
            shapes += [jax.ShapeDtypeStruct((chans * rows + chans * refs, 2 * ZERN), jnp.int16)] * (len(owners) - 1)
        elif owners:
            shapes = [
                jax.ShapeDtypeStruct((rows, 2 * ZERN), jnp.float32),
                jax.ShapeDtypeStruct((stations * refs - rows, 2 * ZERN), jnp.int16),
                jax.ShapeDtypeStruct((refs, stations), jnp.float32),
            ]
        else:
            shapes = [plain]
        before = sums if last else []
        call = pl.pallas_call(
            functools.partial(correlate_kernel, chan, owners, last),
            in_specs=[vmem] * (4 + len(before)),
            out_specs=[vmem] * len(shapes),
            out_shape=shapes,
            scratch_shapes=[
                pltpu.VMEM((parts, refs, times), jnp.float32),
                pltpu.VMEM((refs * 2 * ZERN, 2 * STEP), jnp.bfloat16),
                pltpu.VMEM((refs * 2 * ZERN, 2 * STEP), jnp.bfloat16),
                pltpu.VMEM((refs * 2 * ZERN, parts * stations), jnp.float32),
                pltpu.VMEM(plain.shape, jnp.float32),
            ],
            compiler_params=pltpu.CompilerParams(vmem_limit_bytes=24 * 2**20),
            cost_estimate=pl.CostEstimate(flops=4_300_000_000, bytes_accessed=3_000_000, transcendentals=0),
            name="correlate",
        )
        out = list(call(voltages, *ref_parts[chan], table, *before))
        sums = out if owners else sums + out
    return sums


def collect_kernel(shape, *refs):
    *ins, inverse_ref, out_ref = refs
    chan = lax.axis_index("chan")
    chan_count = lax.axis_size("chan")
    tm_count = len(ins) // chan_count
    chans, own, rows, terms = shape
    for dc in range(chan_count):
        source = jnp.bitwise_xor(chan, dc)
        for c in range(chans):
            total = None
            for at in range(dc, len(ins), chan_count):
                if ins[at].dtype == jnp.int16:
                    begin = c * own * rows
                    level = ins[at][chans * own * rows :, :].astype(jnp.int32).astype(jnp.float32)
                    step = jnp.exp2(level[c * rows : (c + 1) * rows] * (1.0 / LEVELS)) * (1.0 / MOST)
                    part = ins[at][begin : begin + own * rows, :].astype(jnp.int32).astype(jnp.float32)
                    steps = [step[:, at * own + s : at * own + s + 1] for s in range(own)]
                    steps = [jnp.broadcast_to(x, (rows, terms)) for x in steps]
                    part = part * jnp.concatenate(steps, axis=0)
                else:
                    part = ins[at][c].reshape(own * rows, terms)
                total = part if total is None else total + part
            solved = jnp.dot(total, inverse_ref[...], precision=HIGHEST, preferred_element_type=jnp.float32)
            out_ref[:, source * chans + c] = solved.reshape(own, rows, terms)


def collect(pieces, inverse, chan_count, shape):
    chans, stations, refs, terms = shape
    vmem = pl.BlockSpec(memory_space=pltpu.VMEM)
    return pl.pallas_call(
        functools.partial(collect_kernel, shape),
        in_specs=[vmem] * (len(pieces) + 1),
        out_specs=vmem,
        out_shape=jax.ShapeDtypeStruct((stations, chans * chan_count, refs, terms), jnp.float32),
        compiler_params=pltpu.CompilerParams(vmem_limit_bytes=8 * 2**20),
        name="sum_and_solve",
    )(*pieces, inverse)


def on_device(voltages, ref_index, positions, aperture_weight):
    chans, parts, stations, times = voltages.shape
    refs = ref_index.shape[0]
    stat_count = lax.axis_size("stat")
    tm_count = lax.axis_size("tm")
    chan_count = lax.axis_size("chan")
    ref_parts = []
    for picked in pick(ref_index, voltages):
        step = 1
        other = jnp.zeros_like(picked)
        while step < stat_count:
            picked = picked + other if step > 1 else picked
            other = lax.ppermute(picked, "stat", [(i, i ^ step) for i in range(stat_count)])
            step *= 2
        ref_parts.append((picked, other))
    scale = (tm_count * times / CELLS) ** (-0.5)
    table = tables(aperture_weight, positions, scale)
    inverse = gram_inverse(aperture_weight)
    owners = [(dt, dc) for dt in range(tm_count) for dc in range(chan_count)]
    own = stations // len(owners)
    block = (chans, own, refs, 2 * ZERN)
    if own % GROUP == 0 and chans == 2:
        sums = correlate(voltages, ref_parts, table, owners)
    else:
        whole = jnp.stack(correlate(voltages, ref_parts, table, None)).reshape((chans, len(owners)) + block[1:])
        tm, chan = lax.axis_index("tm"), lax.axis_index("chan")
        sums = [
            lax.dynamic_index_in_dim(whole, (tm ^ dt) * chan_count + (chan ^ dc), 1, keepdims=False)
            for dt, dc in owners
        ]
    pieces = []
    for (dt, dc), x in zip(owners, sums):
        if dt or dc:
            pairs = [
                (c * tm_count + t, (c ^ dc) * tm_count + (t ^ dt))
                for c in range(chan_count)
                for t in range(tm_count)
            ]
            x = lax.ppermute(x, ("chan", "tm"), pairs)
        pieces.append(x)
    return collect(pieces, inverse, chan_count, block)


def solution(mesh):
    in_specs = (P("chan", None, "stat", "tm"), P(), P("tm"), P())
    out_specs = P(("stat", "tm", "chan"), None, None, None)
    return jax.shard_map(
        on_device, mesh=mesh, in_specs=in_specs, out_specs=out_specs, check_vma=False
    )
```

```python
import functools
import math

import jax
import jax.numpy as jnp
import numpy as np
from jax import lax
from jax.experimental import pallas as pl
from jax.experimental.pallas import tpu as pltpu
from jax.sharding import PartitionSpec as P

RASTER = 16
ZERN = 64
CELLS = RASTER * RASTER
HIGHEST = lax.Precision.HIGHEST
ROWS = (((1,), (1,)), ((), ()))
GROUP = 16
STEP = 512
LEVELS = 64.0
MOST = 32500.0


def zernike_rows():
    cell_ids = np.arange(CELLS)
    grid_x = ((cell_ids // RASTER - RASTER // 2) + 0.5) / (RASTER / 2.0)
    grid_y = ((cell_ids % RASTER - RASTER // 2) + 0.5) / (RASTER / 2.0)
    radius_sq = grid_x * grid_x + grid_y * grid_y
    in_disk = np.where(radius_sq <= 1.0, 1.0, 0.0)
    rows = []
    degree = 0
    while len(rows) < ZERN:
        for azimuth in range(-degree, degree + 1, 2):
            if len(rows) == ZERN:
                break
            order = abs(azimuth)
            power = (grid_x + 1j * grid_y) ** order
            radial = np.zeros_like(grid_x)
            for k in range((degree - order) // 2 + 1):
                weight = (
                    (-1) ** k
                    * math.factorial(degree - k)
                    / (
                        math.factorial(k)
                        * math.factorial((degree + order) // 2 - k)
                        * math.factorial((degree - order) // 2 - k)
                    )
                )
                radial = radial + weight * radius_sq ** ((degree - 2 * k - order) // 2)
            if azimuth > 0:
                row = radial * power.real * math.sqrt(2.0 * (degree + 1))
            elif azimuth < 0:
                row = radial * power.imag * math.sqrt(2.0 * (degree + 1))
            else:
                row = radial * math.sqrt(degree + 1.0)
            rows.append(row * in_disk)
        degree += 1
    return np.stack(rows).astype(np.float32)


def dft_rows():
    cell_ids = np.arange(CELLS)
    a = cell_ids // RASTER - RASTER // 2
    b = cell_ids % RASTER - RASTER // 2
    phases = (a[:, None] * a[None, :] + b[:, None] * b[None, :]) % RASTER
    angles = phases * (2.0 * math.pi / RASTER)
    return np.concatenate([np.cos(angles), -np.sin(angles)], axis=1).astype(np.float32)


def pick_kernel(index_hbm, volt_hbm, *rest):
    *out_refs, index_ref, volt_ref, rows_ref, index_sem, volt_sem = rest
    chans, parts, stations, _ = volt_ref.shape
    refs = rows_ref.shape[2]
    index_copy = pltpu.make_async_copy(index_hbm, index_ref, index_sem)
    volt_copy = pltpu.make_async_copy(volt_hbm, volt_ref, volt_sem)
    index_copy.start()
    volt_copy.start()
    rows_ref[...] = jnp.zeros_like(rows_ref)
    first = lax.axis_index("stat") * stations
    index_copy.wait()
    volt_copy.wait()
    for r in range(refs):
        local = index_ref[r] - first

        @pl.when(jnp.logical_and(local >= 0, local < stations))
        def _():
            begin = pl.multiple_of(local // GROUP * GROUP, GROUP)
            for c in range(chans):
                for k in range(parts):
                    group = volt_ref[c, k, pl.ds(begin, GROUP), :].astype(jnp.float32)
                    row = lax.broadcasted_iota(jnp.int32, group.shape, 0)
                    group = jnp.where(row == local - begin, group, 0.0)
                    rows_ref[c, k, r : r + 1, :] = jnp.sum(group, axis=0, keepdims=True)

    for c, out_ref in enumerate(out_refs):
        out_ref[...] = rows_ref[c].astype(jnp.bfloat16)


def pick(ref_index, voltages):
    chans, parts, _, times = voltages.shape
    refs = ref_index.shape[0]
    vmem = pl.BlockSpec(memory_space=pltpu.VMEM)
    return pl.pallas_call(
        pick_kernel,
        in_specs=[pl.BlockSpec(memory_space=pltpu.HBM)] * 2,
        out_specs=[vmem] * chans,
        out_shape=[jax.ShapeDtypeStruct((parts, refs, times), jnp.bfloat16)] * chans,
        scratch_shapes=[
            pltpu.SMEM((refs,), jnp.int32),
            pltpu.VMEM(voltages.shape, jnp.bfloat16),
            pltpu.VMEM((chans, parts, refs, times), jnp.float32),
            pltpu.SemaphoreType.DMA,
            pltpu.SemaphoreType.DMA,
        ],
        compiler_params=pltpu.CompilerParams(vmem_limit_bytes=8 * 2**20),
        name="pick_references",
    )(
        pltpu.with_memory_space_constraint(ref_index, pltpu.HBM),
        pltpu.with_memory_space_constraint(voltages, pltpu.HBM),
    )


def invert(gram):
    size = gram.shape[0]
    row = lax.broadcasted_iota(jnp.int32, (size, size), 0)
    lane = lax.broadcasted_iota(jnp.int32, (size, size), 1)
    work = jnp.concatenate([gram, jnp.where(row == lane, 1.0, 0.0)], axis=1)
    shape = (8, 2 * size)
    tiles = [work[t : t + 8] for t in range(0, size, 8)]
    row = lax.broadcasted_iota(jnp.int32, shape, 0)
    for k in range(0, size, 4):
        home, begin = divmod(k, 8)
        r = [jnp.broadcast_to(tiles[home][begin + i : begin + i + 1], shape) for i in range(4)]
        p = {
            (i, j): jnp.broadcast_to(r[i][:, k + j : k + j + 1], shape) for i in range(4) for j in range(i, 4)
        }
        columns = [[jnp.broadcast_to(x[:, k + j : k + j + 1], shape) for j in range(4)] for x in tiles]
        scale = 1.0 / (p[0, 0] * p[1, 1] - p[0, 1] * p[0, 1])
        a00, a01, a11 = p[1, 1] * scale, -p[0, 1] * scale, p[0, 0] * scale
        f00, f01 = a00 * p[0, 2] + a01 * p[1, 2], a00 * p[0, 3] + a01 * p[1, 3]
        f10, f11 = a01 * p[0, 2] + a11 * p[1, 2], a01 * p[0, 3] + a11 * p[1, 3]
        s00 = p[2, 2] - p[0, 2] * f00 - p[1, 2] * f10
        s01 = p[2, 3] - p[0, 2] * f01 - p[1, 2] * f11
        s11 = p[3, 3] - p[0, 3] * f01 - p[1, 3] * f11
        scale = 1.0 / (s00 * s11 - s01 * s01)
        x0, x1 = a00 * r[0] + a01 * r[1], a01 * r[0] + a11 * r[1]
        y0, y1 = r[2] - p[0, 2] * x0 - p[1, 2] * x1, r[3] - p[0, 3] * x0 - p[1, 3] * x1
        n2, n3 = (s11 * y0 - s01 * y1) * scale, (s00 * y1 - s01 * y0) * scale
        new = [x0 - f00 * n2 - f01 * n3, x1 - f10 * n2 - f11 * n3, n2, n3]
        for t, c in enumerate(columns):
            tile = tiles[t] - (c[0] * new[0] + c[1] * new[1]) - (c[2] * new[2] + c[3] * new[3])
            if t == home:
                for i in range(4):
                    tile = jnp.where(row == begin + i, new[i], tile)
            tiles[t] = tile
    return jnp.concatenate(tiles, axis=0)[:, size:]


def split(value, parts):
    pieces = []
    for _ in range(parts):
        piece = value.astype(jnp.bfloat16)
        pieces.append(piece)
        value = value - piece.astype(jnp.float32)
    return pieces


def tables_kernel(scale, weight_ref, zern_ref, dft_ref, pos_ref, out_ref):
    weighted = zern_ref[...] * (weight_ref[...] * scale)
    field = jnp.dot(weighted, dft_ref[...], precision=HIGHEST, preferred_element_type=jnp.float32)
    field = jnp.concatenate([field[:, :CELLS], field[:, CELLS:]], axis=0)
    pieces = split(field, 3)
    times = pos_ref.shape[1]
    cell = lax.broadcasted_iota(jnp.int32, (CELLS, STEP), 0)
    for begin in range(0, times, STEP):
        onehot = jnp.where(cell == pos_ref[:, begin : begin + STEP], 1.0, 0.0).astype(jnp.bfloat16)
        total = jnp.dot(pieces[0], onehot, preferred_element_type=jnp.float32)
        for piece in pieces[1:]:
            total = total + jnp.dot(piece, onehot, preferred_element_type=jnp.float32)
        out_ref[:, begin : begin + STEP] = total


def tables(weight, positions, scale):
    times = positions.shape[0]
    return pl.pallas_call(
        functools.partial(tables_kernel, scale),
        out_shape=jax.ShapeDtypeStruct((2 * ZERN, times), jnp.float32),
        name="projection_per_sample",
        compiler_params=pltpu.CompilerParams(vmem_limit_bytes=12 * 2**20),
        cost_estimate=pl.CostEstimate(flops=4_000_000_000, bytes_accessed=2_000_000, transcendentals=0),
    )(weight.reshape(1, CELLS), jnp.asarray(zernike_rows()), jnp.asarray(dft_rows()), positions.reshape(1, times))


def inverse_kernel(weight_ref, zern_ref, out_ref):
    zern = zern_ref[...]
    gram = lax.dot_general(
        zern * weight_ref[...], zern, ROWS, precision=HIGHEST, preferred_element_type=jnp.float32
    )
    inverse = invert(gram)
    zeros = jnp.zeros_like(inverse)
    out_ref[...] = jnp.concatenate(
        [jnp.concatenate([inverse, zeros], axis=1), jnp.concatenate([zeros, inverse], axis=1)], axis=0
    )


def gram_inverse(weight):
    return pl.pallas_call(
        inverse_kernel,
        out_shape=jax.ShapeDtypeStruct((2 * ZERN, 2 * ZERN), jnp.float32),
        name="gram_inverse",
        compiler_params=pltpu.CompilerParams(vmem_limit_bytes=4 * 2**20),
        cost_estimate=pl.CostEstimate(flops=5_000_000_000, bytes_accessed=200_000, transcendentals=0),
    )(weight.reshape(1, CELLS), jnp.asarray(zernike_rows()))


def correlate_kernel(chan, owners, last, *args):
    (volt_ref, first_ref, second_ref, table_ref), args = args[:4], args[4:]
    before_refs, args = args[: 3 * last], args[3 * last :]
    out_refs, (refs_ref, left_a, left_b, total_ref, stage_ref) = args[:-5], args[-5:]
    _, parts, stations, times = volt_ref.shape
    refs = refs_ref.shape[1]
    steps = times // STEP
    refs_ref[...] = (first_ref[...] + second_ref[...]).astype(jnp.float32)
    own = stations // (len(owners) if owners else 1)
    begins = [0]
    if owners:
        tm, chan_at, chan_count = lax.axis_index("tm"), lax.axis_index("chan"), lax.axis_size("chan")
        begins = [
            pl.multiple_of(
                (jnp.bitwise_xor(tm, dt) * chan_count + jnp.bitwise_xor(chan_at, dc)) * own, own
            )
            for dt, dc in owners
        ]

    def produce(step, left_ref):
        span = pl.ds(step * STEP, STEP)
        for r in range(refs):
            real = refs_ref[0, r : r + 1, span]
            imag = refs_ref[1, r : r + 1, span]
            for half in range(0, ZERN, 16):
                table_r = table_ref[half : half + 16, span]
                table_i = table_ref[ZERN + half : ZERN + half + 16, span]
                for at, value in (
                    (half, real * table_r + imag * table_i),
                    (ZERN + half, real * table_i - imag * table_r),
                ):
                    high, low = split(value, 2)
                    rows = pl.ds(r * 2 * ZERN + at, 16)
                    left_ref[rows, 0:STEP] = high
                    left_ref[rows, STEP : 2 * STEP] = low

    def consume(step, left_ref):
        span = pl.ds(step * STEP, STEP)
        right = jnp.concatenate(
            [volt_ref[chan, k, pl.ds(begin, own), span] for k in range(parts) for begin in begins], axis=0
        )
        right = jnp.concatenate([right, right], axis=1)
        product = lax.dot_general(left_ref[...], right, ROWS, preferred_element_type=jnp.float32)
        if step == 0:
            total_ref[...] = product
        else:
            total_ref[...] += product

    buffers = (left_a, left_b)
    produce(0, buffers[0])
    for step in range(steps):
        if step + 1 < steps:
            produce(step + 1, buffers[(step + 1) % 2])
        consume(step, buffers[step % 2])
    kept = lax.broadcasted_iota(jnp.int32, (1, stations), 1) < own
    levels = []
    for r in range(refs):
        top = total_ref[r * 2 * ZERN : r * 2 * ZERN + ZERN, :]
        low = total_ref[r * 2 * ZERN + ZERN : (r + 1) * 2 * ZERN, :]
        real = top[:, :stations] - low[:, stations:]
        imag = top[:, stations:] + low[:, :stations]
        both = jnp.concatenate([real, imag], axis=0)
        if owners:
            most = jnp.maximum(jnp.max(jnp.abs(both), axis=0, keepdims=True), 1e-30)
            level = jnp.floor(jnp.log2(most) * LEVELS) + 1.0
            levels.append(level)
            rounded = jnp.floor(both * (jnp.exp2(level * (-1.0 / LEVELS)) * MOST) + 0.5)
            both = jnp.where(kept, both, rounded)
        stage_ref[pl.ds(r, stations, stride=refs), :] = both.T
    if not owners:
        out_refs[0][...] = stage_ref[...]
        return
    rows = own * refs
    level = jnp.concatenate(levels, axis=0)
    sent = stage_ref[rows:, :].astype(jnp.int32).astype(jnp.int16)
    if not last:
        out_refs[0][...] = stage_ref[:rows, :]
        out_refs[1][...] = sent
        out_refs[2][...] = level
        return
    out_refs[0][0] = before_refs[0][...]
    out_refs[0][1] = stage_ref[:rows, :]
    levels = jnp.concatenate([before_refs[2][...], level], axis=0).astype(jnp.int32).astype(jnp.int16)
    for i, out_ref in enumerate(out_refs[1:]):
        out_ref[:rows, :] = before_refs[1][i * rows : (i + 1) * rows, :]
        out_ref[rows : 2 * rows, :] = sent[i * rows : (i + 1) * rows]
        out_ref[2 * rows :, :] = levels


def correlate(voltages, ref_parts, table, owners):
    chans, parts, stations, times = voltages.shape
    refs = ref_parts[0][0].shape[1]
    vmem = pl.BlockSpec(memory_space=pltpu.VMEM)
    rows = stations // (len(owners) if owners else 1) * refs
    plain = jax.ShapeDtypeStruct((stations * refs, 2 * ZERN), jnp.float32)
    sums = []
    for chan in range(chans):
        last = owners is not None and chan == chans - 1
        if last:
            shapes = [jax.ShapeDtypeStruct((chans, rows, 2 * ZERN), jnp.float32)]
            shapes += [jax.ShapeDtypeStruct((chans * rows + chans * refs, 2 * ZERN), jnp.int16)] * (len(owners) - 1)
        elif owners:
            shapes = [
                jax.ShapeDtypeStruct((rows, 2 * ZERN), jnp.float32),
                jax.ShapeDtypeStruct((stations * refs - rows, 2 * ZERN), jnp.int16),
                jax.ShapeDtypeStruct((refs, stations), jnp.float32),
            ]
        else:
            shapes = [plain]
        before = sums if last else []
        call = pl.pallas_call(
            functools.partial(correlate_kernel, chan, owners, last),
            in_specs=[vmem] * (4 + len(before)),
            out_specs=[vmem] * len(shapes),
            out_shape=shapes,
            scratch_shapes=[
                pltpu.VMEM((parts, refs, times), jnp.float32),
                pltpu.VMEM((refs * 2 * ZERN, 2 * STEP), jnp.bfloat16),
                pltpu.VMEM((refs * 2 * ZERN, 2 * STEP), jnp.bfloat16),
                pltpu.VMEM((refs * 2 * ZERN, parts * stations), jnp.float32),
                pltpu.VMEM(plain.shape, jnp.float32),
            ],
            compiler_params=pltpu.CompilerParams(vmem_limit_bytes=24 * 2**20),
            cost_estimate=pl.CostEstimate(flops=4_300_000_000, bytes_accessed=3_000_000, transcendentals=0),
            name="correlate",
        )
        out = list(call(voltages, *ref_parts[chan], table, *before))
        sums = out if owners else sums + out
    return sums


def collect_kernel(shape, *refs):
    *ins, inverse_ref, out_ref = refs
    chan = lax.axis_index("chan")
    chan_count = lax.axis_size("chan")
    tm_count = len(ins) // chan_count
    chans, own, rows, terms = shape
    for dc in range(chan_count):
        source = jnp.bitwise_xor(chan, dc)
        for c in range(chans):
            total = None
            for at in range(dc, len(ins), chan_count):
                if ins[at].dtype == jnp.int16:
                    begin = c * own * rows
                    level = ins[at][chans * own * rows :, :].astype(jnp.int32).astype(jnp.float32)
                    step = jnp.exp2(level[c * rows : (c + 1) * rows] * (1.0 / LEVELS)) * (1.0 / MOST)
                    part = ins[at][begin : begin + own * rows, :].astype(jnp.int32).astype(jnp.float32)
                    steps = [step[:, at * own + s : at * own + s + 1] for s in range(own)]
                    steps = [jnp.broadcast_to(x, (rows, terms)) for x in steps]
                    part = part * jnp.concatenate(steps, axis=0)
                else:
                    part = ins[at][c].reshape(own * rows, terms)
                total = part if total is None else total + part
            solved = jnp.dot(total, inverse_ref[...], precision=HIGHEST, preferred_element_type=jnp.float32)
            out_ref[:, source * chans + c] = solved.reshape(own, rows, terms)


def collect(pieces, inverse, chan_count, shape):
    chans, stations, refs, terms = shape
    vmem = pl.BlockSpec(memory_space=pltpu.VMEM)
    return pl.pallas_call(
        functools.partial(collect_kernel, shape),
        in_specs=[vmem] * (len(pieces) + 1),
        out_specs=vmem,
        out_shape=jax.ShapeDtypeStruct((stations, chans * chan_count, refs, terms), jnp.float32),
        compiler_params=pltpu.CompilerParams(vmem_limit_bytes=8 * 2**20),
        name="sum_and_solve",
    )(*pieces, inverse)


def on_device(voltages, ref_index, positions, aperture_weight):
    chans, parts, stations, times = voltages.shape
    refs = ref_index.shape[0]
    stat_count = lax.axis_size("stat")
    tm_count = lax.axis_size("tm")
    chan_count = lax.axis_size("chan")
    ref_parts = []
    for picked in pick(ref_index, voltages):
        step = 1
        other = jnp.zeros_like(picked)
        while step < stat_count:
            picked = picked + other if step > 1 else picked
            other = lax.ppermute(picked, "stat", [(i, i ^ step) for i in range(stat_count)])
            step *= 2
        ref_parts.append((picked, other))
    scale = (tm_count * times / CELLS) ** (-0.5)
    table = tables(aperture_weight, positions, scale)
    inverse = gram_inverse(aperture_weight)
    owners = [(dt, dc) for dt in range(tm_count) for dc in range(chan_count)]
    own = stations // len(owners)
    block = (chans, own, refs, 2 * ZERN)
    if own % GROUP == 0 and chans == 2:
        sums = correlate(voltages, ref_parts, table, owners)
    else:
        whole = jnp.stack(correlate(voltages, ref_parts, table, None)).reshape((chans, len(owners)) + block[1:])
        tm, chan = lax.axis_index("tm"), lax.axis_index("chan")
        sums = [
            lax.dynamic_index_in_dim(whole, (tm ^ dt) * chan_count + (chan ^ dc), 1, keepdims=False)
            for dt, dc in owners
        ]
    pieces = []
    for (dt, dc), x in zip(owners, sums):
        if dt or dc:
            pairs = [
                (c * tm_count + t, (c ^ dc) * tm_count + (t ^ dt))
                for c in range(chan_count)
                for t in range(tm_count)
            ]
            x = lax.ppermute(x, ("chan", "tm"), pairs)
        pieces.append(x)
    return collect(pieces, inverse, chan_count, block)


def solution(mesh):
    in_specs = (P("chan", None, "stat", "tm"), P(), P("tm"), P())
    out_specs = P(("stat", "tm", "chan"), None, None, None)
    return jax.shard_map(
        on_device, mesh=mesh, in_specs=in_specs, out_specs=out_specs, check_vma=False
    )
```

```python
import functools
import math

import jax
import jax.numpy as jnp
import numpy as np
from jax import lax
from jax.experimental import pallas as pl
from jax.experimental.pallas import tpu as pltpu
from jax.sharding import PartitionSpec as P

RASTER = 16
ZERN = 64
CELLS = RASTER * RASTER
HIGHEST = lax.Precision.HIGHEST
ROWS = (((1,), (1,)), ((), ()))
GROUP = 16
STEP = 512
LEVELS = 64.0
MOST = 32500.0


def zernike_rows():
    cell_ids = np.arange(CELLS)
    grid_x = ((cell_ids // RASTER - RASTER // 2) + 0.5) / (RASTER / 2.0)
    grid_y = ((cell_ids % RASTER - RASTER // 2) + 0.5) / (RASTER / 2.0)
    radius_sq = grid_x * grid_x + grid_y * grid_y
    in_disk = np.where(radius_sq <= 1.0, 1.0, 0.0)
    rows = []
    degree = 0
    while len(rows) < ZERN:
        for azimuth in range(-degree, degree + 1, 2):
            if len(rows) == ZERN:
                break
            order = abs(azimuth)
            power = (grid_x + 1j * grid_y) ** order
            radial = np.zeros_like(grid_x)
            for k in range((degree - order) // 2 + 1):
                weight = (
                    (-1) ** k
                    * math.factorial(degree - k)
                    / (
                        math.factorial(k)
                        * math.factorial((degree + order) // 2 - k)
                        * math.factorial((degree - order) // 2 - k)
                    )
                )
                radial = radial + weight * radius_sq ** ((degree - 2 * k - order) // 2)
            if azimuth > 0:
                row = radial * power.real * math.sqrt(2.0 * (degree + 1))
            elif azimuth < 0:
                row = radial * power.imag * math.sqrt(2.0 * (degree + 1))
            else:
                row = radial * math.sqrt(degree + 1.0)
            rows.append(row * in_disk)
        degree += 1
    return np.stack(rows).astype(np.float32)


def dft_rows():
    cell_ids = np.arange(CELLS)
    a = cell_ids // RASTER - RASTER // 2
    b = cell_ids % RASTER - RASTER // 2
    phases = (a[:, None] * a[None, :] + b[:, None] * b[None, :]) % RASTER
    angles = phases * (2.0 * math.pi / RASTER)
    return np.concatenate([np.cos(angles), -np.sin(angles)], axis=1).astype(np.float32)


def owner_and_slot(index_ref, stations):
    owners = [index_ref[r] // stations for r in range(index_ref.shape[0])]
    slots = []
    for r, owner in enumerate(owners):
        slot = jnp.int32(0)
        for other in owners[:r]:
            slot = slot + jnp.where(other == owner, 1, 0)
        slots.append(slot)
    return owners, slots


def pick_kernel(index_hbm, volt_hbm, *rest):
    *out_refs, index_ref, volt_ref, rows_ref, index_sem, volt_sem = rest
    chans, parts, stations, _ = volt_ref.shape
    count = rows_ref.shape[2] // parts
    index_copy = pltpu.make_async_copy(index_hbm, index_ref, index_sem)
    volt_copy = pltpu.make_async_copy(volt_hbm, volt_ref, volt_sem)
    index_copy.start()
    volt_copy.start()
    rows_ref[...] = jnp.zeros_like(rows_ref)
    me = lax.axis_index("stat")
    index_copy.wait()
    owners, slots = owner_and_slot(index_ref, stations)
    volt_copy.wait()
    for r, (owner, slot) in enumerate(zip(owners, slots)):

        @pl.when(owner == me)
        def _():
            local = index_ref[r] - me * stations
            begin = pl.multiple_of(local // GROUP * GROUP, GROUP)
            for c in range(chans):
                for k in range(parts):
                    group = volt_ref[c, k, pl.ds(begin, GROUP), :].astype(jnp.float32)
                    row = lax.broadcasted_iota(jnp.int32, group.shape, 0)
                    group = jnp.where(row == local - begin, group, 0.0)
                    to = pl.ds(k * count + lax.rem(slot, count), 1)
                    rows_ref[slot // count, c, to, :] = jnp.sum(group, axis=0, keepdims=True)

    for i, out_ref in enumerate(out_refs):
        out_ref[...] = rows_ref[i].astype(jnp.bfloat16)


def pick(ref_index, voltages):
    chans, parts, _, times = voltages.shape
    refs = ref_index.shape[0]
    half = (chans, parts * refs // 2, times)
    vmem = pl.BlockSpec(memory_space=pltpu.VMEM)
    return pl.pallas_call(
        pick_kernel,
        in_specs=[pl.BlockSpec(memory_space=pltpu.HBM)] * 2,
        out_specs=[vmem] * 2,
        out_shape=[jax.ShapeDtypeStruct(half, jnp.bfloat16)] * 2,
        scratch_shapes=[
            pltpu.SMEM((refs,), jnp.int32),
            pltpu.VMEM(voltages.shape, jnp.bfloat16),
            pltpu.VMEM((2,) + half, jnp.float32),
            pltpu.SemaphoreType.DMA,
            pltpu.SemaphoreType.DMA,
        ],
        compiler_params=pltpu.CompilerParams(vmem_limit_bytes=8 * 2**20),
        name="pick_references",
    )(
        pltpu.with_memory_space_constraint(ref_index, pltpu.HBM),
        pltpu.with_memory_space_constraint(voltages, pltpu.HBM),
    )


def invert(gram):
    size = gram.shape[0]
    row = lax.broadcasted_iota(jnp.int32, (size, size), 0)
    lane = lax.broadcasted_iota(jnp.int32, (size, size), 1)
    work = jnp.concatenate([gram, jnp.where(row == lane, 1.0, 0.0)], axis=1)
    shape = (8, 2 * size)
    tiles = [work[t : t + 8] for t in range(0, size, 8)]
    row = lax.broadcasted_iota(jnp.int32, shape, 0)
    for k in range(0, size, 4):
        home, begin = divmod(k, 8)
        r = [jnp.broadcast_to(tiles[home][begin + i : begin + i + 1], shape) for i in range(4)]
        p = {
            (i, j): jnp.broadcast_to(r[i][:, k + j : k + j + 1], shape) for i in range(4) for j in range(i, 4)
        }
        columns = [[jnp.broadcast_to(x[:, k + j : k + j + 1], shape) for j in range(4)] for x in tiles]
        scale = 1.0 / (p[0, 0] * p[1, 1] - p[0, 1] * p[0, 1])
        a00, a01, a11 = p[1, 1] * scale, -p[0, 1] * scale, p[0, 0] * scale
        f00, f01 = a00 * p[0, 2] + a01 * p[1, 2], a00 * p[0, 3] + a01 * p[1, 3]
        f10, f11 = a01 * p[0, 2] + a11 * p[1, 2], a01 * p[0, 3] + a11 * p[1, 3]
        s00 = p[2, 2] - p[0, 2] * f00 - p[1, 2] * f10
        s01 = p[2, 3] - p[0, 2] * f01 - p[1, 2] * f11
        s11 = p[3, 3] - p[0, 3] * f01 - p[1, 3] * f11
        scale = 1.0 / (s00 * s11 - s01 * s01)
        x0, x1 = a00 * r[0] + a01 * r[1], a01 * r[0] + a11 * r[1]
        y0, y1 = r[2] - p[0, 2] * x0 - p[1, 2] * x1, r[3] - p[0, 3] * x0 - p[1, 3] * x1
        n2, n3 = (s11 * y0 - s01 * y1) * scale, (s00 * y1 - s01 * y0) * scale
        new = [x0 - f00 * n2 - f01 * n3, x1 - f10 * n2 - f11 * n3, n2, n3]
        for t, c in enumerate(columns):
            tile = tiles[t] - (c[0] * new[0] + c[1] * new[1]) - (c[2] * new[2] + c[3] * new[3])
            if t == home:
                for i in range(4):
                    tile = jnp.where(row == begin + i, new[i], tile)
            tiles[t] = tile
    return jnp.concatenate(tiles, axis=0)[:, size:]


def split(value, parts):
    pieces = []
    for _ in range(parts):
        piece = value.astype(jnp.bfloat16)
        pieces.append(piece)
        value = value - piece.astype(jnp.float32)
    return pieces


def tables_kernel(scale, weight_ref, zern_ref, dft_ref, pos_ref, out_ref):
    weighted = zern_ref[...] * (weight_ref[...] * scale)
    field = jnp.dot(weighted, dft_ref[...], precision=HIGHEST, preferred_element_type=jnp.float32)
    field = jnp.concatenate([field[:, :CELLS], field[:, CELLS:]], axis=0)
    pieces = split(field, 3)
    times = pos_ref.shape[1]
    cell = lax.broadcasted_iota(jnp.int32, (CELLS, STEP), 0)
    for begin in range(0, times, STEP):
        onehot = jnp.where(cell == pos_ref[:, begin : begin + STEP], 1.0, 0.0).astype(jnp.bfloat16)
        total = jnp.dot(pieces[0], onehot, preferred_element_type=jnp.float32)
        for piece in pieces[1:]:
            total = total + jnp.dot(piece, onehot, preferred_element_type=jnp.float32)
        out_ref[:, begin : begin + STEP] = total


def tables(weight, positions, scale):
    times = positions.shape[0]
    return pl.pallas_call(
        functools.partial(tables_kernel, scale),
        out_shape=jax.ShapeDtypeStruct((2 * ZERN, times), jnp.float32),
        name="projection_per_sample",
        compiler_params=pltpu.CompilerParams(vmem_limit_bytes=12 * 2**20),
        cost_estimate=pl.CostEstimate(flops=4_000_000_000, bytes_accessed=2_000_000, transcendentals=0),
    )(weight.reshape(1, CELLS), jnp.asarray(zernike_rows()), jnp.asarray(dft_rows()), positions.reshape(1, times))


def inverse_kernel(weight_ref, zern_ref, out_ref):
    zern = zern_ref[...]
    gram = lax.dot_general(
        zern * weight_ref[...], zern, ROWS, precision=HIGHEST, preferred_element_type=jnp.float32
    )
    inverse = invert(gram)
    zeros = jnp.zeros_like(inverse)
    out_ref[...] = jnp.concatenate(
        [jnp.concatenate([inverse, zeros], axis=1), jnp.concatenate([zeros, inverse], axis=1)], axis=0
    )


def gram_inverse(weight):
    return pl.pallas_call(
        inverse_kernel,
        out_shape=jax.ShapeDtypeStruct((2 * ZERN, 2 * ZERN), jnp.float32),
        name="gram_inverse",
        compiler_params=pltpu.CompilerParams(vmem_limit_bytes=4 * 2**20),
        cost_estimate=pl.CostEstimate(flops=5_000_000_000, bytes_accessed=200_000, transcendentals=0),
    )(weight.reshape(1, CELLS), jnp.asarray(zernike_rows()))


def correlate_kernel(owners, stat_count, index_ref, volt_ref, *args):
    part_refs, args = args[:stat_count], args[stat_count:]
    extra_ref, table_ref, *out_refs = args[:-7]
    refs_ref, left_a, left_b, total_ref, stage_ref, more_ref, more_sem = args[-7:]
    chans, parts, stations, times = volt_ref.shape
    refs = index_ref.shape[0]
    count = refs // 2
    steps = times // STEP
    me = lax.axis_index("stat")
    places, more = [], jnp.int32(0)
    for owner, slot in zip(*owner_and_slot(index_ref, stations)):
        places.append(((slot // count) * stat_count + lax.rem(me - owner + stat_count, stat_count), lax.rem(slot, count)))
        more = more + slot // count
    for i, part_ref in enumerate(part_refs):
        refs_ref[i] = part_ref[...].astype(jnp.float32)

    @pl.when(more > 0)
    def _():
        copy = pltpu.make_async_copy(extra_ref, more_ref, more_sem)
        copy.start()
        copy.wait()
        for i in range(stat_count):
            refs_ref[stat_count + i] = more_ref[i].astype(jnp.float32)

    own = stations // (len(owners) if owners else 1)
    begins = [0]
    if owners:
        tm, chan_at, chan_count = lax.axis_index("tm"), lax.axis_index("chan"), lax.axis_size("chan")
        begins = [
            pl.multiple_of(
                (jnp.bitwise_xor(tm, dt) * chan_count + jnp.bitwise_xor(chan_at, dc)) * own, own
            )
            for dt, dc in owners
        ]

    def produce(chan, step, left_ref):
        span = pl.ds(step * STEP, STEP)
        for r, (place, row) in enumerate(places):
            real = refs_ref[place, chan, pl.ds(row, 1), span]
            imag = refs_ref[place, chan, pl.ds(count + row, 1), span]
            for half in range(0, ZERN, 16):
                table_r = table_ref[half : half + 16, span]
                table_i = table_ref[ZERN + half : ZERN + half + 16, span]
                for at, value in (
                    (half, real * table_r + imag * table_i),
                    (ZERN + half, real * table_i - imag * table_r),
                ):
                    high, low = split(value, 2)
                    rows = pl.ds(r * 2 * ZERN + at, 16)
                    left_ref[rows, 0:STEP] = high
                    left_ref[rows, STEP : 2 * STEP] = low

    def consume(chan, step, left_ref):
        span = pl.ds(step * STEP, STEP)
        right = jnp.concatenate(
            [volt_ref[chan, k, pl.ds(begin, own), span] for k in range(parts) for begin in begins], axis=0
        )
        right = jnp.concatenate([right, right], axis=1)
        product = lax.dot_general(left_ref[...], right, ROWS, preferred_element_type=jnp.float32)
        if step == 0:
            total_ref[...] = product
        else:
            total_ref[...] += product

    def finish(chan):
        kept = lax.broadcasted_iota(jnp.int32, (1, stations), 1) < own
        levels = []
        for r in range(refs):
            top = total_ref[r * 2 * ZERN : r * 2 * ZERN + ZERN, :]
            low = total_ref[r * 2 * ZERN + ZERN : (r + 1) * 2 * ZERN, :]
            real = top[:, :stations] - low[:, stations:]
            imag = top[:, stations:] + low[:, :stations]
            both = jnp.concatenate([real, imag], axis=0)
            if owners:
                most = jnp.maximum(jnp.max(jnp.abs(both), axis=0, keepdims=True), 1e-30)
                level = jnp.floor(jnp.log2(most) * LEVELS) + 1.0
                levels.append(level)
                rounded = jnp.floor(both * (jnp.exp2(level * (-1.0 / LEVELS)) * MOST) + 0.5)
                both = jnp.where(kept, both, rounded)
            stage_ref[pl.ds(r, stations, stride=refs), :] = both.T
        if not owners:
            out_refs[0][chan] = stage_ref[...]
            return
        rows = own * refs
        out_refs[0][chan] = stage_ref[:rows, :]
        level = jnp.concatenate(levels, axis=0).astype(jnp.int32).astype(jnp.int16)
        for i, out_ref in enumerate(out_refs[1:]):
            block = stage_ref[(i + 1) * rows : (i + 2) * rows, :]
            out_ref[chan * rows : (chan + 1) * rows, :] = block.astype(jnp.int32).astype(jnp.int16)
            out_ref[chans * rows + chan * refs : chans * rows + (chan + 1) * refs, :] = level

    order = [(chan, step) for chan in range(chans) for step in range(steps)]
    buffers = (left_a, left_b)
    produce(*order[0], buffers[0])
    for i, (chan, step) in enumerate(order):
        if i + 1 < len(order):
            produce(*order[i + 1], buffers[(i + 1) % 2])
        consume(chan, step, buffers[i % 2])
        if step == steps - 1:
            finish(chan)


def correlate(ref_index, voltages, ref_parts, extra, table, owners):
    chans, parts, stations, times = voltages.shape
    refs = ref_index.shape[0]
    vmem = pl.BlockSpec(memory_space=pltpu.VMEM)
    rows = stations // (len(owners) if owners else 1) * refs
    shapes = [jax.ShapeDtypeStruct((chans, rows, 2 * ZERN), jnp.float32)]
    if owners:
        shapes += [jax.ShapeDtypeStruct((chans * (rows + refs), 2 * ZERN), jnp.int16)] * (len(owners) - 1)
    return pl.pallas_call(
        functools.partial(correlate_kernel, owners, len(ref_parts)),
        in_specs=[pl.BlockSpec(memory_space=pltpu.SMEM)]
        + [vmem] * (1 + len(ref_parts))
        + [pl.BlockSpec(memory_space=pltpu.HBM), vmem],
        out_specs=[vmem] * len(shapes),
        out_shape=shapes,
        scratch_shapes=[
            pltpu.VMEM((2 * len(ref_parts),) + ref_parts[0].shape, jnp.float32),
            pltpu.VMEM((refs * 2 * ZERN, 2 * STEP), jnp.bfloat16),
            pltpu.VMEM((refs * 2 * ZERN, 2 * STEP), jnp.bfloat16),
            pltpu.VMEM((refs * 2 * ZERN, parts * stations), jnp.float32),
            pltpu.VMEM((stations * refs, 2 * ZERN), jnp.float32),
            pltpu.VMEM(extra.shape, extra.dtype),
            pltpu.SemaphoreType.DMA,
        ],
        compiler_params=pltpu.CompilerParams(vmem_limit_bytes=24 * 2**20),
        cost_estimate=pl.CostEstimate(flops=8_600_000_000, bytes_accessed=5_000_000, transcendentals=0),
        name="correlate",
    )(ref_index, voltages, *ref_parts, pltpu.with_memory_space_constraint(extra, pltpu.HBM), table)


def unwritten(shape, dtype):
    return pl.pallas_call(
        lambda out_ref: None,
        out_specs=pl.BlockSpec(memory_space=pltpu.HBM),
        out_shape=jax.ShapeDtypeStruct(shape, dtype),
        name="no_second_round",
    )()


def collect_kernel(order, shape, *refs):
    *ins, inverse_ref, out_ref = refs
    ins = [ins[list(order).index(at)] for at in range(len(ins))]
    chan = lax.axis_index("chan")
    chan_count = lax.axis_size("chan")
    tm_count = len(ins) // chan_count
    chans, own, rows, terms = shape
    for dc in range(chan_count):
        source = jnp.bitwise_xor(chan, dc)
        for c in range(chans):
            total = None
            for at in range(dc, len(ins), chan_count):
                if ins[at].dtype == jnp.int16:
                    begin = c * own * rows
                    level = ins[at][chans * own * rows :, :].astype(jnp.int32).astype(jnp.float32)
                    step = jnp.exp2(level[c * rows : (c + 1) * rows] * (1.0 / LEVELS)) * (1.0 / MOST)
                    part = ins[at][begin : begin + own * rows, :].astype(jnp.int32).astype(jnp.float32)
                    steps = [step[:, at * own + s : at * own + s + 1] for s in range(own)]
                    steps = [jnp.broadcast_to(x, (rows, terms)) for x in steps]
                    part = part * jnp.concatenate(steps, axis=0)
                else:
                    part = ins[at][c].reshape(own * rows, terms)
                total = part if total is None else total + part
            solved = jnp.dot(total, inverse_ref[...], precision=HIGHEST, preferred_element_type=jnp.float32)
            out_ref[:, source * chans + c] = solved.reshape(own, rows, terms)


def collect(pieces, order, inverse, chan_count, shape):
    chans, stations, refs, terms = shape
    vmem = pl.BlockSpec(memory_space=pltpu.VMEM)
    return pl.pallas_call(
        functools.partial(collect_kernel, order, shape),
        in_specs=[vmem] * (len(pieces) + 1),
        out_specs=vmem,
        out_shape=jax.ShapeDtypeStruct((stations, chans * chan_count, refs, terms), jnp.float32),
        compiler_params=pltpu.CompilerParams(vmem_limit_bytes=8 * 2**20),
        name="sum_and_solve",
    )(*pieces, inverse)


def on_device(voltages, ref_index, positions, aperture_weight):
    chans, parts, stations, times = voltages.shape
    refs = ref_index.shape[0]
    stat_count = lax.axis_size("stat")
    tm_count = lax.axis_size("tm")
    chan_count = lax.axis_size("chan")
    first, second = pick(ref_index, voltages)

    def to_all(own):
        shifts = [[(i, (i + k) % stat_count) for i in range(stat_count)] for k in range(1, stat_count)]
        return [own] + [lax.ppermute(own, "stat", pairs) for pairs in shifts]

    ref_parts = to_all(first)
    holders = ref_index // stations
    most = jnp.max(jnp.sum(holders[:, None] == jnp.arange(stat_count)[None, :], axis=0))
    second, *ref_parts = lax.optimization_barrier((second, *ref_parts))
    extra = lax.cond(
        most > refs // 2,
        lambda own: jnp.stack(to_all(own)),
        lambda own: unwritten((stat_count,) + own.shape, own.dtype),
        second,
    )
    scale = (tm_count * times / CELLS) ** (-0.5)
    table = tables(aperture_weight, positions, scale)
    inverse = gram_inverse(aperture_weight)
    owners = [(dt, dc) for dt in range(tm_count) for dc in range(chan_count)]
    order = [0, 4, 5, 2, 3, 1, 6, 7] if len(owners) == 8 else range(len(owners))
    own = stations // len(owners)
    block = (chans, own, refs, 2 * ZERN)
    if own % GROUP == 0:
        sums = correlate(ref_index, voltages, ref_parts, extra, table, owners)
    else:
        whole = correlate(ref_index, voltages, ref_parts, extra, table, None)[0]
        whole = whole.reshape((chans, len(owners)) + block[1:])
        tm, chan = lax.axis_index("tm"), lax.axis_index("chan")
        sums = [
            lax.dynamic_index_in_dim(whole, (tm ^ dt) * chan_count + (chan ^ dc), 1, keepdims=False)
            for dt, dc in owners
        ]
    pieces = []
    for at in order:
        x = sums[at]
        if at:
            dt, dc = owners[at]
            pairs = [
                (c * tm_count + t, (c ^ dc) * tm_count + (t ^ dt))
                for c in range(chan_count)
                for t in range(tm_count)
            ]
            x = lax.ppermute(x, ("chan", "tm"), pairs)
        pieces.append(x)
    return collect(pieces, order, inverse, chan_count, block)


def solution(mesh):
    in_specs = (P("chan", None, "stat", "tm"), P(), P("tm"), P())
    out_specs = P(("stat", "tm", "chan"), None, None, None)
    return jax.shard_map(
        on_device, mesh=mesh, in_specs=in_specs, out_specs=out_specs, check_vma=False
    )
```

```python
import functools
import math

import jax
import jax.numpy as jnp
import numpy as np
from jax import lax
from jax.experimental import pallas as pl
from jax.experimental.pallas import tpu as pltpu
from jax.sharding import PartitionSpec as P

RASTER = 16
ZERN = 64
CELLS = RASTER * RASTER
HIGHEST = lax.Precision.HIGHEST
ROWS = (((1,), (1,)), ((), ()))
GROUP = 16
STEP = 512
LEVELS = 64.0
MOST = 32500.0


def zernike_rows():
    cell_ids = np.arange(CELLS)
    grid_x = ((cell_ids // RASTER - RASTER // 2) + 0.5) / (RASTER / 2.0)
    grid_y = ((cell_ids % RASTER - RASTER // 2) + 0.5) / (RASTER / 2.0)
    radius_sq = grid_x * grid_x + grid_y * grid_y
    in_disk = np.where(radius_sq <= 1.0, 1.0, 0.0)
    rows = []
    degree = 0
    while len(rows) < ZERN:
        for azimuth in range(-degree, degree + 1, 2):
            if len(rows) == ZERN:
                break
            order = abs(azimuth)
            power = (grid_x + 1j * grid_y) ** order
            radial = np.zeros_like(grid_x)
            for k in range((degree - order) // 2 + 1):
                weight = (
                    (-1) ** k
                    * math.factorial(degree - k)
                    / (
                        math.factorial(k)
                        * math.factorial((degree + order) // 2 - k)
                        * math.factorial((degree - order) // 2 - k)
                    )
                )
                radial = radial + weight * radius_sq ** ((degree - 2 * k - order) // 2)
            if azimuth > 0:
                row = radial * power.real * math.sqrt(2.0 * (degree + 1))
            elif azimuth < 0:
                row = radial * power.imag * math.sqrt(2.0 * (degree + 1))
            else:
                row = radial * math.sqrt(degree + 1.0)
            rows.append(row * in_disk)
        degree += 1
    return np.stack(rows).astype(np.float32)


def dft_rows():
    cell_ids = np.arange(CELLS)
    a = cell_ids // RASTER - RASTER // 2
    b = cell_ids % RASTER - RASTER // 2
    phases = (a[:, None] * a[None, :] + b[:, None] * b[None, :]) % RASTER
    angles = phases * (2.0 * math.pi / RASTER)
    return np.concatenate([np.cos(angles), -np.sin(angles)], axis=1).astype(np.float32)


def owner_and_slot(index_ref, stations):
    owners = [index_ref[r] // stations for r in range(index_ref.shape[0])]
    slots = []
    for r, owner in enumerate(owners):
        slot = jnp.int32(0)
        for other in owners[:r]:
            slot = slot + jnp.where(other == owner, 1, 0)
        slots.append(slot)
    return owners, slots


def pick_kernel(index_hbm, volt_hbm, *rest):
    *out_refs, index_ref, volt_ref, rows_ref, index_sem, volt_sem = rest
    chans, parts, stations, _ = volt_ref.shape
    count = rows_ref.shape[2] // parts
    index_copy = pltpu.make_async_copy(index_hbm, index_ref, index_sem)
    volt_copy = pltpu.make_async_copy(volt_hbm, volt_ref, volt_sem)
    index_copy.start()
    volt_copy.start()
    rows_ref[...] = jnp.zeros_like(rows_ref)
    me = lax.axis_index("stat")
    index_copy.wait()
    owners, slots = owner_and_slot(index_ref, stations)
    volt_copy.wait()
    for r, (owner, slot) in enumerate(zip(owners, slots)):

        @pl.when(owner == me)
        def _():
            local = index_ref[r] - me * stations
            begin = pl.multiple_of(local // GROUP * GROUP, GROUP)
            for c in range(chans):
                for k in range(parts):
                    group = volt_ref[c, k, pl.ds(begin, GROUP), :].astype(jnp.float32)
                    row = lax.broadcasted_iota(jnp.int32, group.shape, 0)
                    group = jnp.where(row == local - begin, group, 0.0)
                    to = pl.ds(k * count + lax.rem(slot, count), 1)
                    rows_ref[slot // count, c, to, :] = jnp.sum(group, axis=0, keepdims=True)

    for i, out_ref in enumerate(out_refs):
        out_ref[...] = rows_ref[i].astype(jnp.bfloat16)


def pick(ref_index, voltages):
    chans, parts, _, times = voltages.shape
    refs = ref_index.shape[0]
    half = (chans, parts * refs // 2, times)
    vmem = pl.BlockSpec(memory_space=pltpu.VMEM)
    return pl.pallas_call(
        pick_kernel,
        in_specs=[pl.BlockSpec(memory_space=pltpu.HBM)] * 2,
        out_specs=[vmem] * 2,
        out_shape=[jax.ShapeDtypeStruct(half, jnp.bfloat16)] * 2,
        scratch_shapes=[
            pltpu.SMEM((refs,), jnp.int32),
            pltpu.VMEM(voltages.shape, jnp.bfloat16),
            pltpu.VMEM((2,) + half, jnp.float32),
            pltpu.SemaphoreType.DMA,
            pltpu.SemaphoreType.DMA,
        ],
        compiler_params=pltpu.CompilerParams(vmem_limit_bytes=8 * 2**20),
        name="pick_references",
    )(
        pltpu.with_memory_space_constraint(ref_index, pltpu.HBM),
        pltpu.with_memory_space_constraint(voltages, pltpu.HBM),
    )


def invert(gram):
    size = gram.shape[0]
    row = lax.broadcasted_iota(jnp.int32, (size, size), 0)
    lane = lax.broadcasted_iota(jnp.int32, (size, size), 1)
    work = jnp.concatenate([gram, jnp.where(row == lane, 1.0, 0.0)], axis=1)
    shape = (8, 2 * size)
    tiles = [work[t : t + 8] for t in range(0, size, 8)]
    row = lax.broadcasted_iota(jnp.int32, shape, 0)
    for k in range(0, size, 4):
        home, begin = divmod(k, 8)
        r = [jnp.broadcast_to(tiles[home][begin + i : begin + i + 1], shape) for i in range(4)]
        p = {
            (i, j): jnp.broadcast_to(r[i][:, k + j : k + j + 1], shape) for i in range(4) for j in range(i, 4)
        }
        columns = [[jnp.broadcast_to(x[:, k + j : k + j + 1], shape) for j in range(4)] for x in tiles]
        scale = 1.0 / (p[0, 0] * p[1, 1] - p[0, 1] * p[0, 1])
        a00, a01, a11 = p[1, 1] * scale, -p[0, 1] * scale, p[0, 0] * scale
        f00, f01 = a00 * p[0, 2] + a01 * p[1, 2], a00 * p[0, 3] + a01 * p[1, 3]
        f10, f11 = a01 * p[0, 2] + a11 * p[1, 2], a01 * p[0, 3] + a11 * p[1, 3]
        s00 = p[2, 2] - p[0, 2] * f00 - p[1, 2] * f10
        s01 = p[2, 3] - p[0, 2] * f01 - p[1, 2] * f11
        s11 = p[3, 3] - p[0, 3] * f01 - p[1, 3] * f11
        scale = 1.0 / (s00 * s11 - s01 * s01)
        x0, x1 = a00 * r[0] + a01 * r[1], a01 * r[0] + a11 * r[1]
        y0, y1 = r[2] - p[0, 2] * x0 - p[1, 2] * x1, r[3] - p[0, 3] * x0 - p[1, 3] * x1
        n2, n3 = (s11 * y0 - s01 * y1) * scale, (s00 * y1 - s01 * y0) * scale
        new = [x0 - f00 * n2 - f01 * n3, x1 - f10 * n2 - f11 * n3, n2, n3]
        for t, c in enumerate(columns):
            tile = tiles[t] - (c[0] * new[0] + c[1] * new[1]) - (c[2] * new[2] + c[3] * new[3])
            if t == home:
                for i in range(4):
                    tile = jnp.where(row == begin + i, new[i], tile)
            tiles[t] = tile
    return jnp.concatenate(tiles, axis=0)[:, size:]


def split(value, parts):
    pieces = []
    for _ in range(parts):
        piece = value.astype(jnp.bfloat16)
        pieces.append(piece)
        value = value - piece.astype(jnp.float32)
    return pieces


def tables_kernel(scale, weight_ref, zern_ref, dft_ref, pos_ref, out_ref):
    weighted = zern_ref[...] * (weight_ref[...] * scale)
    field = jnp.dot(weighted, dft_ref[...], precision=HIGHEST, preferred_element_type=jnp.float32)
    field = jnp.concatenate([field[:, :CELLS], field[:, CELLS:]], axis=0)
    pieces = split(field, 3)
    times = pos_ref.shape[1]
    cell = lax.broadcasted_iota(jnp.int32, (CELLS, STEP), 0)
    for begin in range(0, times, STEP):
        onehot = jnp.where(cell == pos_ref[:, begin : begin + STEP], 1.0, 0.0).astype(jnp.bfloat16)
        total = jnp.dot(pieces[0], onehot, preferred_element_type=jnp.float32)
        for piece in pieces[1:]:
            total = total + jnp.dot(piece, onehot, preferred_element_type=jnp.float32)
        out_ref[:, begin : begin + STEP] = total


def tables(weight, positions, scale):
    times = positions.shape[0]
    return pl.pallas_call(
        functools.partial(tables_kernel, scale),
        out_shape=jax.ShapeDtypeStruct((2 * ZERN, times), jnp.float32),
        name="projection_per_sample",
        compiler_params=pltpu.CompilerParams(vmem_limit_bytes=12 * 2**20),
        cost_estimate=pl.CostEstimate(flops=4_000_000_000, bytes_accessed=2_000_000, transcendentals=0),
    )(weight.reshape(1, CELLS), jnp.asarray(zernike_rows()), jnp.asarray(dft_rows()), positions.reshape(1, times))


def inverse_kernel(weight_ref, zern_ref, out_ref):
    zern = zern_ref[...]
    gram = lax.dot_general(
        zern * weight_ref[...], zern, ROWS, precision=HIGHEST, preferred_element_type=jnp.float32
    )
    inverse = invert(gram)
    zeros = jnp.zeros_like(inverse)
    out_ref[...] = jnp.concatenate(
        [jnp.concatenate([inverse, zeros], axis=1), jnp.concatenate([zeros, inverse], axis=1)], axis=0
    )


def gram_inverse(weight):
    return pl.pallas_call(
        inverse_kernel,
        out_shape=jax.ShapeDtypeStruct((2 * ZERN, 2 * ZERN), jnp.float32),
        name="gram_inverse",
        compiler_params=pltpu.CompilerParams(vmem_limit_bytes=4 * 2**20),
        cost_estimate=pl.CostEstimate(flops=5_000_000_000, bytes_accessed=200_000, transcendentals=0),
    )(weight.reshape(1, CELLS), jnp.asarray(zernike_rows()))


def shift_order(stat_count):
    return [0, 2, 3, 1] if stat_count == 4 else list(range(stat_count))


def correlate_kernel(owners, stat_count, index_ref, volt_ref, *args):
    part_refs, args = args[:stat_count], args[stat_count:]
    extra_ref, table_ref, *out_refs = args[:-7]
    refs_ref, left_a, left_b, total_ref, stage_ref, more_ref, more_sem = args[-7:]
    chans, parts, stations, times = volt_ref.shape
    refs = index_ref.shape[0]
    count = refs // 2
    steps = times // STEP
    me = lax.axis_index("stat")
    places, more = [], jnp.int32(0)
    for owner, slot in zip(*owner_and_slot(index_ref, stations)):
        shift, place = jnp.bitwise_xor(me, owner), jnp.int32(0)
        for i, k in enumerate(shift_order(stat_count)):
            place = jnp.where(shift == k, i, place)
        places.append(((slot // count) * stat_count + place, lax.rem(slot, count)))
        more = more + slot // count
    for i, part_ref in enumerate(part_refs):
        refs_ref[i] = part_ref[...].astype(jnp.float32)

    @pl.when(more > 0)
    def _():
        copy = pltpu.make_async_copy(extra_ref, more_ref, more_sem)
        copy.start()
        copy.wait()
        for i in range(stat_count):
            refs_ref[stat_count + i] = more_ref[i].astype(jnp.float32)

    own = stations // (len(owners) if owners else 1)
    begins = [0]
    if owners:
        tm, chan_at, chan_count = lax.axis_index("tm"), lax.axis_index("chan"), lax.axis_size("chan")
        begins = [
            pl.multiple_of(
                (jnp.bitwise_xor(tm, dt) * chan_count + jnp.bitwise_xor(chan_at, dc)) * own, own
            )
            for dt, dc in owners
        ]

    def produce(chan, step, left_ref):
        span = pl.ds(step * STEP, STEP)
        for r, (place, row) in enumerate(places):
            real = refs_ref[place, chan, pl.ds(row, 1), span]
            imag = refs_ref[place, chan, pl.ds(count + row, 1), span]
            for half in range(0, ZERN, 16):
                table_r = table_ref[half : half + 16, span]
                table_i = table_ref[ZERN + half : ZERN + half + 16, span]
                for at, value in (
                    (half, real * table_r + imag * table_i),
                    (ZERN + half, real * table_i - imag * table_r),
                ):
                    high, low = split(value, 2)
                    left_ref[pl.ds(r * 2 * ZERN + at, 16), :] = high
                    left_ref[pl.ds((refs + r) * 2 * ZERN + at, 16), :] = low

    def consume(chan, step, left_ref):
        span = pl.ds(step * STEP, STEP)
        right = jnp.concatenate(
            [volt_ref[chan, k, pl.ds(begin, own), span] for k in range(parts) for begin in begins], axis=0
        )
        product = lax.dot_general(left_ref[...], right, ROWS, preferred_element_type=jnp.float32)
        product = product[: refs * 2 * ZERN] + product[refs * 2 * ZERN :]
        if step == 0:
            total_ref[...] = product
        else:
            total_ref[...] += product

    def finish(chan):
        kept = lax.broadcasted_iota(jnp.int32, (1, stations), 1) < own
        levels = []
        for r in range(refs):
            top = total_ref[r * 2 * ZERN : r * 2 * ZERN + ZERN, :]
            low = total_ref[r * 2 * ZERN + ZERN : (r + 1) * 2 * ZERN, :]
            real = top[:, :stations] - low[:, stations:]
            imag = top[:, stations:] + low[:, :stations]
            both = jnp.concatenate([real, imag], axis=0)
            if owners:
                most = jnp.maximum(jnp.max(jnp.abs(both), axis=0, keepdims=True), 1e-30)
                level = jnp.floor(jnp.log2(most) * LEVELS) + 1.0
                levels.append(level)
                rounded = jnp.floor(both * (jnp.exp2(level * (-1.0 / LEVELS)) * MOST) + 0.5)
                both = jnp.where(kept, both, rounded)
            stage_ref[pl.ds(r, stations, stride=refs), :] = both.T
        if not owners:
            out_refs[0][chan] = stage_ref[: stations * refs, :]
            return
        rows = own * refs
        out_refs[0][chan] = stage_ref[:rows, :]
        level = jnp.concatenate(levels, axis=0).astype(jnp.int32).astype(jnp.int16)
        for i, out_ref in enumerate(out_refs[1:]):
            block = stage_ref[(i + 1) * rows : (i + 2) * rows, :]
            out_ref[chan * rows : (chan + 1) * rows, :] = block.astype(jnp.int32).astype(jnp.int16)
            out_ref[chans * rows + chan * refs : chans * rows + (chan + 1) * refs, :] = level

    order = [(chan, step) for chan in range(chans) for step in range(steps)]
    buffers = (left_a, left_b)
    produce(*order[0], buffers[0])
    for i, (chan, step) in enumerate(order):
        if i + 1 < len(order):
            produce(*order[i + 1], buffers[(i + 1) % 2])
        consume(chan, step, buffers[i % 2])
        if step == steps - 1:
            finish(chan)


def correlate(ref_index, voltages, ref_parts, extra, table, owners):
    chans, parts, stations, times = voltages.shape
    refs = ref_index.shape[0]
    vmem = pl.BlockSpec(memory_space=pltpu.VMEM)
    rows = stations // (len(owners) if owners else 1) * refs
    shapes = [jax.ShapeDtypeStruct((chans, rows, 2 * ZERN), jnp.float32)]
    if owners:
        shapes += [jax.ShapeDtypeStruct((chans * (rows + refs), 2 * ZERN), jnp.int16)] * (len(owners) - 1)
    return pl.pallas_call(
        functools.partial(correlate_kernel, owners, len(ref_parts)),
        in_specs=[pl.BlockSpec(memory_space=pltpu.SMEM)]
        + [vmem] * (1 + len(ref_parts))
        + [pl.BlockSpec(memory_space=pltpu.HBM), vmem],
        out_specs=[vmem] * len(shapes),
        out_shape=shapes,
        scratch_shapes=[
            pltpu.VMEM((2 * len(ref_parts),) + ref_parts[0].shape, jnp.float32),
            pltpu.VMEM((2 * refs * 2 * ZERN, STEP), jnp.bfloat16),
            pltpu.VMEM((2 * refs * 2 * ZERN, STEP), jnp.bfloat16),
            pltpu.VMEM((refs * 2 * ZERN, parts * stations), jnp.float32),
            pltpu.VMEM(((stations + 1) * refs, 2 * ZERN), jnp.float32),
            pltpu.VMEM(extra.shape, extra.dtype),
            pltpu.SemaphoreType.DMA,
        ],
        compiler_params=pltpu.CompilerParams(vmem_limit_bytes=24 * 2**20),
        cost_estimate=pl.CostEstimate(flops=8_600_000_000, bytes_accessed=5_000_000, transcendentals=0),
        name="correlate",
    )(ref_index, voltages, *ref_parts, pltpu.with_memory_space_constraint(extra, pltpu.HBM), table)


def unwritten(shape, dtype):
    return pl.pallas_call(
        lambda out_ref: None,
        out_specs=pl.BlockSpec(memory_space=pltpu.HBM),
        out_shape=jax.ShapeDtypeStruct(shape, dtype),
        name="no_second_round",
    )()


def collect_kernel(order, shape, *refs):
    *ins, inverse_ref, out_ref, stage_ref, sems = refs
    ins = [ins[list(order).index(at)] for at in range(len(ins))]
    chan = lax.axis_index("chan")
    chan_count = lax.axis_size("chan")
    tm_count = len(ins) // chan_count
    chans, own, rows, terms = shape
    copies = []
    for dc in range(chan_count):
        source = jnp.bitwise_xor(chan, dc)
        for c in range(chans):
            total = None
            for at in range(dc, len(ins), chan_count):
                if ins[at].dtype == jnp.int16:
                    begin = c * own * rows
                    level = ins[at][chans * own * rows :, :].astype(jnp.int32).astype(jnp.float32)
                    step = jnp.exp2(level[c * rows : (c + 1) * rows] * (1.0 / LEVELS)) * (1.0 / MOST)
                    part = ins[at][begin : begin + own * rows, :].astype(jnp.int32).astype(jnp.float32)
                    steps = [step[:, at * own + s : at * own + s + 1] for s in range(own)]
                    steps = [jnp.broadcast_to(x, (rows, terms)) for x in steps]
                    part = part * jnp.concatenate(steps, axis=0)
                else:
                    part = ins[at][c].reshape(own * rows, terms)
                total = part if total is None else total + part
            solved = jnp.dot(total, inverse_ref[...], precision=HIGHEST, preferred_element_type=jnp.float32)
            stage_ref[dc, :, c] = solved.reshape(own, rows, terms)
        to = out_ref.at[:, pl.ds(source * chans, chans)]
        copies.append(pltpu.make_async_copy(stage_ref.at[dc], to, sems.at[dc]))
        copies[-1].start()
    for copy in copies:
        copy.wait()


def collect(pieces, order, inverse, chan_count, shape):
    chans, stations, refs, terms = shape
    vmem = pl.BlockSpec(memory_space=pltpu.VMEM)
    return pl.pallas_call(
        functools.partial(collect_kernel, order, shape),
        in_specs=[vmem] * (len(pieces) + 1),
        out_specs=pl.BlockSpec(memory_space=pltpu.HBM),
        out_shape=jax.ShapeDtypeStruct((stations, chans * chan_count, refs, terms), jnp.float32),
        scratch_shapes=[
            pltpu.VMEM((chan_count, stations, chans, refs, terms), jnp.float32),
            pltpu.SemaphoreType.DMA((chan_count,)),
        ],
        compiler_params=pltpu.CompilerParams(vmem_limit_bytes=8 * 2**20),
        name="sum_and_solve",
    )(*pieces, inverse)


def on_device(voltages, ref_index, positions, aperture_weight):
    chans, parts, stations, times = voltages.shape
    refs = ref_index.shape[0]
    stat_count = lax.axis_size("stat")
    tm_count = lax.axis_size("tm")
    chan_count = lax.axis_size("chan")
    first, second = pick(ref_index, voltages)

    def to_all(own):
        shifts = [[(i, i ^ k) for i in range(stat_count)] for k in shift_order(stat_count)[1:]]
        return [own] + [lax.ppermute(own, "stat", pairs) for pairs in shifts]

    ref_parts = to_all(first)
    holders = ref_index // stations
    most = jnp.max(jnp.sum(holders[:, None] == jnp.arange(stat_count)[None, :], axis=0))
    second, *ref_parts = lax.optimization_barrier((second, *ref_parts))
    extra = lax.cond(
        most > refs // 2,
        lambda own: jnp.stack(to_all(own)),
        lambda own: unwritten((stat_count,) + own.shape, own.dtype),
        second,
    )
    scale = (tm_count * times / CELLS) ** (-0.5)
    table = tables(aperture_weight, positions, scale)
    inverse = gram_inverse(aperture_weight)
    owners = [(dt, dc) for dt in range(tm_count) for dc in range(chan_count)]
    order = [0, 4, 5, 2, 3, 1, 6, 7] if len(owners) == 8 else range(len(owners))
    own = stations // len(owners)
    block = (chans, own, refs, 2 * ZERN)
    if own % GROUP == 0:
        sums = correlate(ref_index, voltages, ref_parts, extra, table, owners)
    else:
        whole = correlate(ref_index, voltages, ref_parts, extra, table, None)[0]
        whole = whole.reshape((chans, len(owners)) + block[1:])
        tm, chan = lax.axis_index("tm"), lax.axis_index("chan")
        sums = [
            lax.dynamic_index_in_dim(whole, (tm ^ dt) * chan_count + (chan ^ dc), 1, keepdims=False)
            for dt, dc in owners
        ]
    pieces = []
    for at in order:
        x = sums[at]
        if at:
            dt, dc = owners[at]
            pairs = [
                (c * tm_count + t, (c ^ dc) * tm_count + (t ^ dt))
                for c in range(chan_count)
                for t in range(tm_count)
            ]
            x = lax.ppermute(x, ("chan", "tm"), pairs)
        pieces.append(x)
    return collect(pieces, order, inverse, chan_count, block)


def solution(mesh):
    in_specs = (P("chan", None, "stat", "tm"), P(), P("tm"), P())
    out_specs = P(("stat", "tm", "chan"), None, None, None)
    return jax.shard_map(
        on_device, mesh=mesh, in_specs=in_specs, out_specs=out_specs, check_vma=False
    )
```

```python
import functools
import math

import jax
import jax.numpy as jnp
import numpy as np
from jax import lax
from jax.experimental import pallas as pl
from jax.experimental.pallas import tpu as pltpu
from jax.sharding import PartitionSpec as P

RASTER = 16
ZERN = 64
CELLS = RASTER * RASTER
HIGHEST = lax.Precision.HIGHEST
ROWS = (((1,), (1,)), ((), ()))
GROUP = 16
STEP = 512
LEVELS = 64.0
MOST = 32500.0


def zernike_rows():
    cell_ids = np.arange(CELLS)
    grid_x = ((cell_ids // RASTER - RASTER // 2) + 0.5) / (RASTER / 2.0)
    grid_y = ((cell_ids % RASTER - RASTER // 2) + 0.5) / (RASTER / 2.0)
    radius_sq = grid_x * grid_x + grid_y * grid_y
    in_disk = np.where(radius_sq <= 1.0, 1.0, 0.0)
    rows = []
    degree = 0
    while len(rows) < ZERN:
        for azimuth in range(-degree, degree + 1, 2):
            if len(rows) == ZERN:
                break
            order = abs(azimuth)
            power = (grid_x + 1j * grid_y) ** order
            radial = np.zeros_like(grid_x)
            for k in range((degree - order) // 2 + 1):
                weight = (
                    (-1) ** k
                    * math.factorial(degree - k)
                    / (
                        math.factorial(k)
                        * math.factorial((degree + order) // 2 - k)
                        * math.factorial((degree - order) // 2 - k)
                    )
                )
                radial = radial + weight * radius_sq ** ((degree - 2 * k - order) // 2)
            if azimuth > 0:
                row = radial * power.real * math.sqrt(2.0 * (degree + 1))
            elif azimuth < 0:
                row = radial * power.imag * math.sqrt(2.0 * (degree + 1))
            else:
                row = radial * math.sqrt(degree + 1.0)
            rows.append(row * in_disk)
        degree += 1
    return np.stack(rows).astype(np.float32)


def dft_rows():
    cell_ids = np.arange(CELLS)
    a = cell_ids // RASTER - RASTER // 2
    b = cell_ids % RASTER - RASTER // 2
    phases = (a[:, None] * a[None, :] + b[:, None] * b[None, :]) % RASTER
    angles = phases * (2.0 * math.pi / RASTER)
    return np.concatenate([np.cos(angles), -np.sin(angles)], axis=1).astype(np.float32)


def owner_and_slot(index_ref, stations):
    owners = [index_ref[r] // stations for r in range(index_ref.shape[0])]
    slots = []
    for r, owner in enumerate(owners):
        slot = jnp.int32(0)
        for other in owners[:r]:
            slot = slot + jnp.where(other == owner, 1, 0)
        slots.append(slot)
    return owners, slots


def pick_kernel(index_hbm, volt_hbm, *rest):
    *out_refs, index_ref, volt_ref, rows_ref, index_sem, volt_sem = rest
    chans, parts, stations, _ = volt_ref.shape
    count = rows_ref.shape[2] // parts
    index_copy = pltpu.make_async_copy(index_hbm, index_ref, index_sem)
    volt_copy = pltpu.make_async_copy(volt_hbm, volt_ref, volt_sem)
    index_copy.start()
    volt_copy.start()
    rows_ref[...] = jnp.zeros_like(rows_ref)
    me = lax.axis_index("stat")
    index_copy.wait()
    owners, slots = owner_and_slot(index_ref, stations)
    volt_copy.wait()
    for r, (owner, slot) in enumerate(zip(owners, slots)):

        @pl.when(owner == me)
        def _():
            local = index_ref[r] - me * stations
            begin = pl.multiple_of(local // GROUP * GROUP, GROUP)
            for c in range(chans):
                for k in range(parts):
                    group = volt_ref[c, k, pl.ds(begin, GROUP), :].astype(jnp.float32)
                    row = lax.broadcasted_iota(jnp.int32, group.shape, 0)
                    group = jnp.where(row == local - begin, group, 0.0)
                    to = pl.ds(k * count + lax.rem(slot, count), 1)
                    rows_ref[slot // count, c, to, :] = jnp.sum(group, axis=0, keepdims=True)

    for i, out_ref in enumerate(out_refs):
        out_ref[...] = rows_ref[i].astype(jnp.bfloat16)


def pick(ref_index, voltages):
    chans, parts, _, times = voltages.shape
    refs = ref_index.shape[0]
    half = (chans, parts * refs // 2, times)
    vmem = pl.BlockSpec(memory_space=pltpu.VMEM)
    return pl.pallas_call(
        pick_kernel,
        in_specs=[pl.BlockSpec(memory_space=pltpu.HBM)] * 2,
        out_specs=[vmem] * 2,
        out_shape=[jax.ShapeDtypeStruct(half, jnp.bfloat16)] * 2,
        scratch_shapes=[
            pltpu.SMEM((refs,), jnp.int32),
            pltpu.VMEM(voltages.shape, jnp.bfloat16),
            pltpu.VMEM((2,) + half, jnp.float32),
            pltpu.SemaphoreType.DMA,
            pltpu.SemaphoreType.DMA,
        ],
        compiler_params=pltpu.CompilerParams(vmem_limit_bytes=8 * 2**20),
        name="pick_references",
    )(
        pltpu.with_memory_space_constraint(ref_index, pltpu.HBM),
        pltpu.with_memory_space_constraint(voltages, pltpu.HBM),
    )


def invert(gram):
    size = gram.shape[0]
    row = lax.broadcasted_iota(jnp.int32, (size, size), 0)
    lane = lax.broadcasted_iota(jnp.int32, (size, size), 1)
    work = jnp.concatenate([gram, jnp.where(row == lane, 1.0, 0.0)], axis=1)
    shape = (8, 2 * size)
    tiles = [work[t : t + 8] for t in range(0, size, 8)]
    row = lax.broadcasted_iota(jnp.int32, shape, 0)
    for k in range(0, size, 4):
        home, begin = divmod(k, 8)
        r = [jnp.broadcast_to(tiles[home][begin + i : begin + i + 1], shape) for i in range(4)]
        p = {
            (i, j): jnp.broadcast_to(r[i][:, k + j : k + j + 1], shape) for i in range(4) for j in range(i, 4)
        }
        columns = [[jnp.broadcast_to(x[:, k + j : k + j + 1], shape) for j in range(4)] for x in tiles]
        scale = 1.0 / (p[0, 0] * p[1, 1] - p[0, 1] * p[0, 1])
        a00, a01, a11 = p[1, 1] * scale, -p[0, 1] * scale, p[0, 0] * scale
        f00, f01 = a00 * p[0, 2] + a01 * p[1, 2], a00 * p[0, 3] + a01 * p[1, 3]
        f10, f11 = a01 * p[0, 2] + a11 * p[1, 2], a01 * p[0, 3] + a11 * p[1, 3]
        s00 = p[2, 2] - p[0, 2] * f00 - p[1, 2] * f10
        s01 = p[2, 3] - p[0, 2] * f01 - p[1, 2] * f11
        s11 = p[3, 3] - p[0, 3] * f01 - p[1, 3] * f11
        scale = 1.0 / (s00 * s11 - s01 * s01)
        x0, x1 = a00 * r[0] + a01 * r[1], a01 * r[0] + a11 * r[1]
        y0, y1 = r[2] - p[0, 2] * x0 - p[1, 2] * x1, r[3] - p[0, 3] * x0 - p[1, 3] * x1
        n2, n3 = (s11 * y0 - s01 * y1) * scale, (s00 * y1 - s01 * y0) * scale
        new = [x0 - f00 * n2 - f01 * n3, x1 - f10 * n2 - f11 * n3, n2, n3]
        for t, c in enumerate(columns):
            tile = tiles[t] - (c[0] * new[0] + c[1] * new[1]) - (c[2] * new[2] + c[3] * new[3])
            if t == home:
                for i in range(4):
                    tile = jnp.where(row == begin + i, new[i], tile)
            tiles[t] = tile
    return jnp.concatenate(tiles, axis=0)[:, size:]


def split(value, parts):
    pieces = []
    for _ in range(parts):
        piece = value.astype(jnp.bfloat16)
        pieces.append(piece)
        value = value - piece.astype(jnp.float32)
    return pieces


def tables_kernel(scale, weight_ref, zern_ref, dft_ref, pos_ref, out_ref):
    weighted = zern_ref[...] * (weight_ref[...] * scale)
    field = jnp.dot(weighted, dft_ref[...], precision=HIGHEST, preferred_element_type=jnp.float32)
    field = jnp.concatenate([field[:, :CELLS], field[:, CELLS:]], axis=0)
    pieces = split(field, 3)
    times = pos_ref.shape[1]
    cell = lax.broadcasted_iota(jnp.int32, (CELLS, STEP), 0)
    for begin in range(0, times, STEP):
        onehot = jnp.where(cell == pos_ref[:, begin : begin + STEP], 1.0, 0.0).astype(jnp.bfloat16)
        total = jnp.dot(pieces[0], onehot, preferred_element_type=jnp.float32)
        for piece in pieces[1:]:
            total = total + jnp.dot(piece, onehot, preferred_element_type=jnp.float32)
        out_ref[:, begin : begin + STEP] = total


def tables(weight, positions, scale):
    times = positions.shape[0]
    return pl.pallas_call(
        functools.partial(tables_kernel, scale),
        out_shape=jax.ShapeDtypeStruct((2 * ZERN, times), jnp.float32),
        name="projection_per_sample",
        compiler_params=pltpu.CompilerParams(vmem_limit_bytes=12 * 2**20),
        cost_estimate=pl.CostEstimate(flops=4_000_000_000, bytes_accessed=2_000_000, transcendentals=0),
    )(weight.reshape(1, CELLS), jnp.asarray(zernike_rows()), jnp.asarray(dft_rows()), positions.reshape(1, times))


def inverse_kernel(weight_ref, zern_ref, out_ref):
    zern = zern_ref[...]
    gram = lax.dot_general(
        zern * weight_ref[...], zern, ROWS, precision=HIGHEST, preferred_element_type=jnp.float32
    )
    inverse = invert(gram)
    zeros = jnp.zeros_like(inverse)
    inverse = jnp.concatenate(
        [jnp.concatenate([inverse, zeros], axis=1), jnp.concatenate([zeros, inverse], axis=1)], axis=0
    )
    high, low = split(inverse, 2)
    out_ref[...] = jnp.concatenate([high, high, low], axis=0)


def gram_inverse(weight):
    return pl.pallas_call(
        inverse_kernel,
        out_shape=jax.ShapeDtypeStruct((6 * ZERN, 2 * ZERN), jnp.bfloat16),
        name="gram_inverse",
        compiler_params=pltpu.CompilerParams(vmem_limit_bytes=4 * 2**20),
        cost_estimate=pl.CostEstimate(flops=5_000_000_000, bytes_accessed=200_000, transcendentals=0),
    )(weight.reshape(1, CELLS), jnp.asarray(zernike_rows()))


def shift_order(stat_count):
    return [0, 2, 3, 1] if stat_count == 4 else list(range(stat_count))


def correlate_kernel(owners, stat_count, index_ref, volt_ref, *args):
    part_refs, args = args[:stat_count], args[stat_count:]
    extra_ref, table_ref, *out_refs = args[:-7]
    refs_ref, left_a, left_b, total_ref, stage_ref, more_ref, more_sem = args[-7:]
    chans, parts, stations, times = volt_ref.shape
    refs = index_ref.shape[0]
    count = refs // 2
    steps = times // STEP
    me = lax.axis_index("stat")
    places, more = [], jnp.int32(0)
    for owner, slot in zip(*owner_and_slot(index_ref, stations)):
        shift, place = jnp.bitwise_xor(me, owner), jnp.int32(0)
        for i, k in enumerate(shift_order(stat_count)):
            place = jnp.where(shift == k, i, place)
        places.append(((slot // count) * stat_count + place, lax.rem(slot, count)))
        more = more + slot // count
    for i, part_ref in enumerate(part_refs):
        refs_ref[i] = part_ref[...].astype(jnp.float32)

    @pl.when(more > 0)
    def _():
        copy = pltpu.make_async_copy(extra_ref, more_ref, more_sem)
        copy.start()
        copy.wait()
        for i in range(stat_count):
            refs_ref[stat_count + i] = more_ref[i].astype(jnp.float32)

    own = stations // (len(owners) if owners else 1)
    begins = [0]
    if owners:
        tm, chan_at, chan_count = lax.axis_index("tm"), lax.axis_index("chan"), lax.axis_size("chan")
        begins = [
            pl.multiple_of(
                (jnp.bitwise_xor(tm, dt) * chan_count + jnp.bitwise_xor(chan_at, dc)) * own, own
            )
            for dt, dc in owners
        ]

    def produce(chan, step, left_ref):
        span = pl.ds(step * STEP, STEP)
        for r, (place, row) in enumerate(places):
            real = refs_ref[place, chan, pl.ds(row, 1), span]
            imag = refs_ref[place, chan, pl.ds(count + row, 1), span]
            for half in range(0, ZERN, 16):
                table_r = table_ref[half : half + 16, span]
                table_i = table_ref[ZERN + half : ZERN + half + 16, span]
                for at, value in (
                    (half, real * table_r + imag * table_i),
                    (ZERN + half, real * table_i - imag * table_r),
                ):
                    high, low = split(value, 2)
                    left_ref[pl.ds(r * 2 * ZERN + at, 16), :] = high
                    left_ref[pl.ds((refs + r) * 2 * ZERN + at, 16), :] = low

    def consume(chan, step, left_ref):
        span = pl.ds(step * STEP, STEP)
        right = jnp.concatenate(
            [volt_ref[chan, k, pl.ds(begin, own), span] for k in range(parts) for begin in begins], axis=0
        )
        product = lax.dot_general(left_ref[...], right, ROWS, preferred_element_type=jnp.float32)
        product = product[: refs * 2 * ZERN] + product[refs * 2 * ZERN :]
        if step == 0:
            total_ref[...] = product
        else:
            total_ref[...] += product

    def finish(chan):
        kept = lax.broadcasted_iota(jnp.int32, (1, stations), 1) < own
        levels = []
        for r in range(refs):
            top = total_ref[r * 2 * ZERN : r * 2 * ZERN + ZERN, :]
            low = total_ref[r * 2 * ZERN + ZERN : (r + 1) * 2 * ZERN, :]
            real = top[:, :stations] - low[:, stations:]
            imag = top[:, stations:] + low[:, :stations]
            both = jnp.concatenate([real, imag], axis=0)
            if owners:
                most = jnp.maximum(jnp.max(jnp.abs(both), axis=0, keepdims=True), 1e-30)
                level = jnp.floor(jnp.log2(most) * LEVELS) + 1.0
                levels.append(level)
                rounded = jnp.floor(both * (jnp.exp2(level * (-1.0 / LEVELS)) * MOST) + 0.5)
                both = jnp.where(kept, both, rounded)
            stage_ref[pl.ds(r, stations, stride=refs), :] = both.T
        if not owners:
            out_refs[0][chan] = stage_ref[: stations * refs, :]
            return
        rows = own * refs
        out_refs[0][chan] = stage_ref[:rows, :]
        level = jnp.concatenate(levels, axis=0).astype(jnp.int32).astype(jnp.int16)
        for i, out_ref in enumerate(out_refs[1:]):
            block = stage_ref[(i + 1) * rows : (i + 2) * rows, :]
            out_ref[chan * rows : (chan + 1) * rows, :] = block.astype(jnp.int32).astype(jnp.int16)
            out_ref[chans * rows + chan * refs : chans * rows + (chan + 1) * refs, :] = level

    order = [(chan, step) for chan in range(chans) for step in range(steps)]
    buffers = (left_a, left_b)
    produce(*order[0], buffers[0])
    for i, (chan, step) in enumerate(order):
        if i + 1 < len(order):
            produce(*order[i + 1], buffers[(i + 1) % 2])
        consume(chan, step, buffers[i % 2])
        if step == steps - 1:
            finish(chan)


def correlate(ref_index, voltages, ref_parts, extra, table, owners):
    chans, parts, stations, times = voltages.shape
    refs = ref_index.shape[0]
    vmem = pl.BlockSpec(memory_space=pltpu.VMEM)
    rows = stations // (len(owners) if owners else 1) * refs
    shapes = [jax.ShapeDtypeStruct((chans, rows, 2 * ZERN), jnp.float32)]
    if owners:
        shapes += [jax.ShapeDtypeStruct((chans * (rows + refs), 2 * ZERN), jnp.int16)] * (len(owners) - 1)
    return pl.pallas_call(
        functools.partial(correlate_kernel, owners, len(ref_parts)),
        in_specs=[pl.BlockSpec(memory_space=pltpu.SMEM)]
        + [vmem] * (1 + len(ref_parts))
        + [pl.BlockSpec(memory_space=pltpu.HBM), vmem],
        out_specs=[vmem] * len(shapes),
        out_shape=shapes,
        scratch_shapes=[
            pltpu.VMEM((2 * len(ref_parts),) + ref_parts[0].shape, jnp.float32),
            pltpu.VMEM((2 * refs * 2 * ZERN, STEP), jnp.bfloat16),
            pltpu.VMEM((2 * refs * 2 * ZERN, STEP), jnp.bfloat16),
            pltpu.VMEM((refs * 2 * ZERN, parts * stations), jnp.float32),
            pltpu.VMEM(((stations + 1) * refs, 2 * ZERN), jnp.float32),
            pltpu.VMEM(extra.shape, extra.dtype),
            pltpu.SemaphoreType.DMA,
        ],
        compiler_params=pltpu.CompilerParams(vmem_limit_bytes=24 * 2**20),
        cost_estimate=pl.CostEstimate(flops=8_600_000_000, bytes_accessed=5_000_000, transcendentals=0),
        name="correlate",
    )(ref_index, voltages, *ref_parts, pltpu.with_memory_space_constraint(extra, pltpu.HBM), table)


def unwritten(shape, dtype):
    return pl.pallas_call(
        lambda out_ref: None,
        out_specs=pl.BlockSpec(memory_space=pltpu.HBM),
        out_shape=jax.ShapeDtypeStruct(shape, dtype),
        name="no_second_round",
    )()


def collect_kernel(order, shape, *refs):
    *ins, inverse_ref, out_ref, stage_ref, sems = refs
    ins = [ins[list(order).index(at)] for at in range(len(ins))]
    chan = lax.axis_index("chan")
    chan_count = lax.axis_size("chan")
    tm_count = len(ins) // chan_count
    chans, own, rows, terms = shape
    copies = []
    for dc in range(chan_count):
        source = jnp.bitwise_xor(chan, dc)
        for c in range(chans):
            total = None
            for at in range(dc, len(ins), chan_count):
                if ins[at].dtype == jnp.int16:
                    begin = c * own * rows
                    level = ins[at][chans * own * rows :, :].astype(jnp.int32).astype(jnp.float32)
                    step = jnp.exp2(level[c * rows : (c + 1) * rows] * (1.0 / LEVELS)) * (1.0 / MOST)
                    part = ins[at][begin : begin + own * rows, :].astype(jnp.int32).astype(jnp.float32)
                    steps = [step[:, at * own + s : at * own + s + 1] for s in range(own)]
                    steps = [jnp.broadcast_to(x, (rows, terms)) for x in steps]
                    part = part * jnp.concatenate(steps, axis=0)
                else:
                    part = ins[at][c].reshape(own * rows, terms)
                total = part if total is None else total + part
            high, low = split(total, 2)
            pieces = jnp.concatenate([high, low, high], axis=1)
            solved = jnp.dot(pieces, inverse_ref[...], preferred_element_type=jnp.float32)
            stage_ref[dc, :, c] = solved.reshape(own, rows, terms)
        to = out_ref.at[:, pl.ds(source * chans, chans)]
        copies.append(pltpu.make_async_copy(stage_ref.at[dc], to, sems.at[dc]))
        copies[-1].start()
    for copy in copies:
        copy.wait()


def collect(pieces, order, inverse, chan_count, shape):
    chans, stations, refs, terms = shape
    vmem = pl.BlockSpec(memory_space=pltpu.VMEM)
    return pl.pallas_call(
        functools.partial(collect_kernel, order, shape),
        in_specs=[vmem] * (len(pieces) + 1),
        out_specs=pl.BlockSpec(memory_space=pltpu.HBM),
        out_shape=jax.ShapeDtypeStruct((stations, chans * chan_count, refs, terms), jnp.float32),
        scratch_shapes=[
            pltpu.VMEM((chan_count, stations, chans, refs, terms), jnp.float32),
            pltpu.SemaphoreType.DMA((chan_count,)),
        ],
        compiler_params=pltpu.CompilerParams(vmem_limit_bytes=8 * 2**20),
        name="sum_and_solve",
    )(*pieces, inverse)


def on_device(voltages, ref_index, positions, aperture_weight):
    chans, parts, stations, times = voltages.shape
    refs = ref_index.shape[0]
    stat_count = lax.axis_size("stat")
    tm_count = lax.axis_size("tm")
    chan_count = lax.axis_size("chan")
    first, second = pick(ref_index, voltages)

    def to_all(own):
        shifts = [[(i, i ^ k) for i in range(stat_count)] for k in shift_order(stat_count)[1:]]
        return [own] + [lax.ppermute(own, "stat", pairs) for pairs in shifts]

    ref_parts = to_all(first)
    holders = ref_index // stations
    most = jnp.max(jnp.sum(holders[:, None] == jnp.arange(stat_count)[None, :], axis=0))
    second, *ref_parts = lax.optimization_barrier((second, *ref_parts))
    extra = lax.cond(
        most > refs // 2,
        lambda own: jnp.stack(to_all(own)),
        lambda own: unwritten((stat_count,) + own.shape, own.dtype),
        second,
    )
    scale = (tm_count * times / CELLS) ** (-0.5)
    table = tables(aperture_weight, positions, scale)
    inverse = gram_inverse(aperture_weight)
    owners = [(dt, dc) for dt in range(tm_count) for dc in range(chan_count)]
    order = [0, 4, 5, 2, 3, 1, 6, 7] if len(owners) == 8 else range(len(owners))
    own = stations // len(owners)
    block = (chans, own, refs, 2 * ZERN)
    if own % GROUP == 0:
        sums = correlate(ref_index, voltages, ref_parts, extra, table, owners)
    else:
        whole = correlate(ref_index, voltages, ref_parts, extra, table, None)[0]
        whole = whole.reshape((chans, len(owners)) + block[1:])
        tm, chan = lax.axis_index("tm"), lax.axis_index("chan")
        sums = [
            lax.dynamic_index_in_dim(whole, (tm ^ dt) * chan_count + (chan ^ dc), 1, keepdims=False)
            for dt, dc in owners
        ]
    pieces = []
    for at in order:
        x = sums[at]
        if at:
            dt, dc = owners[at]
            pairs = [
                (c * tm_count + t, (c ^ dc) * tm_count + (t ^ dt))
                for c in range(chan_count)
                for t in range(tm_count)
            ]
            x = lax.ppermute(x, ("chan", "tm"), pairs)
        pieces.append(x)
    return collect(pieces, order, inverse, chan_count, block)


def solution(mesh):
    in_specs = (P("chan", None, "stat", "tm"), P(), P("tm"), P())
    out_specs = P(("stat", "tm", "chan"), None, None, None)
    return jax.shard_map(
        on_device, mesh=mesh, in_specs=in_specs, out_specs=out_specs, check_vma=False
    )
```

```python
import functools
import math

import jax
import jax.numpy as jnp
import numpy as np
from jax import lax
from jax.experimental import pallas as pl
from jax.experimental.pallas import tpu as pltpu
from jax.sharding import PartitionSpec as P

RASTER = 16
ZERN = 64
CELLS = RASTER * RASTER
HIGHEST = lax.Precision.HIGHEST
ROWS = (((1,), (1,)), ((), ()))
GROUP = 16
STEP = 512
LEVELS = 64.0
MOST = 32500.0


def zernike_rows():
    cell_ids = np.arange(CELLS)
    grid_x = ((cell_ids // RASTER - RASTER // 2) + 0.5) / (RASTER / 2.0)
    grid_y = ((cell_ids % RASTER - RASTER // 2) + 0.5) / (RASTER / 2.0)
    radius_sq = grid_x * grid_x + grid_y * grid_y
    in_disk = np.where(radius_sq <= 1.0, 1.0, 0.0)
    rows = []
    degree = 0
    while len(rows) < ZERN:
        for azimuth in range(-degree, degree + 1, 2):
            if len(rows) == ZERN:
                break
            order = abs(azimuth)
            power = (grid_x + 1j * grid_y) ** order
            radial = np.zeros_like(grid_x)
            for k in range((degree - order) // 2 + 1):
                weight = (
                    (-1) ** k
                    * math.factorial(degree - k)
                    / (
                        math.factorial(k)
                        * math.factorial((degree + order) // 2 - k)
                        * math.factorial((degree - order) // 2 - k)
                    )
                )
                radial = radial + weight * radius_sq ** ((degree - 2 * k - order) // 2)
            if azimuth > 0:
                row = radial * power.real * math.sqrt(2.0 * (degree + 1))
            elif azimuth < 0:
                row = radial * power.imag * math.sqrt(2.0 * (degree + 1))
            else:
                row = radial * math.sqrt(degree + 1.0)
            rows.append(row * in_disk)
        degree += 1
    return np.stack(rows).astype(np.float32)


def dft_rows():
    cell_ids = np.arange(CELLS)
    a = cell_ids // RASTER - RASTER // 2
    b = cell_ids % RASTER - RASTER // 2
    phases = (a[:, None] * a[None, :] + b[:, None] * b[None, :]) % RASTER
    angles = phases * (2.0 * math.pi / RASTER)
    return np.concatenate([np.cos(angles), -np.sin(angles)], axis=1).astype(np.float32)


def owner_and_slot(index_ref, stations):
    owners = [index_ref[r] // stations for r in range(index_ref.shape[0])]
    slots = []
    for r, owner in enumerate(owners):
        slot = jnp.int32(0)
        for other in owners[:r]:
            slot = slot + jnp.where(other == owner, 1, 0)
        slots.append(slot)
    return owners, slots


def pick_kernel(index_hbm, volt_hbm, *rest):
    *out_refs, index_ref, volt_ref, rows_ref, group_ref, index_sem, volt_sem = rest
    chans, parts, stations, _ = volt_ref.shape
    count = rows_ref.shape[2] // parts
    index_copy = pltpu.make_async_copy(index_hbm, index_ref, index_sem)
    volt_copy = pltpu.make_async_copy(volt_hbm, volt_ref, volt_sem)
    index_copy.start()
    volt_copy.start()
    rows_ref[...] = jnp.zeros_like(rows_ref)
    me = lax.axis_index("stat")
    index_copy.wait()
    owners, slots = owner_and_slot(index_ref, stations)
    volt_copy.wait()
    for r, (owner, slot) in enumerate(zip(owners, slots)):

        @pl.when(owner == me)
        def _():
            local = index_ref[r] - me * stations
            begin = pl.multiple_of(local // GROUP * GROUP, GROUP)
            for c in range(chans):
                for k in range(parts):
                    group = volt_ref[c, k, pl.ds(begin, GROUP), :].astype(jnp.float32)
                    group_ref[c, k] = group
            for c in range(chans):
                for k in range(parts):
                    to = pl.ds(k * count + lax.rem(slot, count), 1)
                    rows_ref[slot // count, c, to, :] = group_ref[c, k, pl.ds(local - begin, 1), :]

    for i, out_ref in enumerate(out_refs):
        out_ref[...] = rows_ref[i].astype(jnp.bfloat16)


def pick(ref_index, voltages):
    chans, parts, _, times = voltages.shape
    refs = ref_index.shape[0]
    half = (chans, parts * refs // 2, times)
    vmem = pl.BlockSpec(memory_space=pltpu.VMEM)
    return pl.pallas_call(
        pick_kernel,
        in_specs=[pl.BlockSpec(memory_space=pltpu.HBM)] * 2,
        out_specs=[vmem] * 2,
        out_shape=[jax.ShapeDtypeStruct(half, jnp.bfloat16)] * 2,
        scratch_shapes=[
            pltpu.SMEM((refs,), jnp.int32),
            pltpu.VMEM(voltages.shape, jnp.bfloat16),
            pltpu.VMEM((2,) + half, jnp.float32),
            pltpu.VMEM((chans, parts, GROUP, times), jnp.float32),
            pltpu.SemaphoreType.DMA,
            pltpu.SemaphoreType.DMA,
        ],
        compiler_params=pltpu.CompilerParams(vmem_limit_bytes=8 * 2**20),
        name="pick_references",
    )(
        pltpu.with_memory_space_constraint(ref_index, pltpu.HBM),
        pltpu.with_memory_space_constraint(voltages, pltpu.HBM),
    )


def invert(gram):
    size = gram.shape[0]
    row = lax.broadcasted_iota(jnp.int32, (size, size), 0)
    lane = lax.broadcasted_iota(jnp.int32, (size, size), 1)
    work = jnp.concatenate([gram, jnp.where(row == lane, 1.0, 0.0)], axis=1)
    shape = (8, 2 * size)
    tiles = [work[t : t + 8] for t in range(0, size, 8)]
    row = lax.broadcasted_iota(jnp.int32, shape, 0)
    for k in range(0, size, 4):
        home, begin = divmod(k, 8)
        r = [jnp.broadcast_to(tiles[home][begin + i : begin + i + 1], shape) for i in range(4)]
        p = {
            (i, j): jnp.broadcast_to(r[i][:, k + j : k + j + 1], shape) for i in range(4) for j in range(i, 4)
        }
        columns = [[jnp.broadcast_to(x[:, k + j : k + j + 1], shape) for j in range(4)] for x in tiles]
        scale = 1.0 / (p[0, 0] * p[1, 1] - p[0, 1] * p[0, 1])
        a00, a01, a11 = p[1, 1] * scale, -p[0, 1] * scale, p[0, 0] * scale
        f00, f01 = a00 * p[0, 2] + a01 * p[1, 2], a00 * p[0, 3] + a01 * p[1, 3]
        f10, f11 = a01 * p[0, 2] + a11 * p[1, 2], a01 * p[0, 3] + a11 * p[1, 3]
        s00 = p[2, 2] - p[0, 2] * f00 - p[1, 2] * f10
        s01 = p[2, 3] - p[0, 2] * f01 - p[1, 2] * f11
        s11 = p[3, 3] - p[0, 3] * f01 - p[1, 3] * f11
        scale = 1.0 / (s00 * s11 - s01 * s01)
        x0, x1 = a00 * r[0] + a01 * r[1], a01 * r[0] + a11 * r[1]
        y0, y1 = r[2] - p[0, 2] * x0 - p[1, 2] * x1, r[3] - p[0, 3] * x0 - p[1, 3] * x1
        n2, n3 = (s11 * y0 - s01 * y1) * scale, (s00 * y1 - s01 * y0) * scale
        new = [x0 - f00 * n2 - f01 * n3, x1 - f10 * n2 - f11 * n3, n2, n3]
        for t, c in enumerate(columns):
            tile = tiles[t] - (c[0] * new[0] + c[1] * new[1]) - (c[2] * new[2] + c[3] * new[3])
            if t == home:
                for i in range(4):
                    tile = jnp.where(row == begin + i, new[i], tile)
            tiles[t] = tile
    return jnp.concatenate(tiles, axis=0)[:, size:]


def split(value, parts):
    pieces = []
    for _ in range(parts):
        piece = value.astype(jnp.bfloat16)
        pieces.append(piece)
        value = value - piece.astype(jnp.float32)
    return pieces


def tables_kernel(scale, weight_ref, zern_ref, dft_ref, pos_ref, out_ref):
    weighted = zern_ref[...] * (weight_ref[...] * scale)
    field = jnp.dot(weighted, dft_ref[...], precision=HIGHEST, preferred_element_type=jnp.float32)
    field = jnp.concatenate([field[:, :CELLS], field[:, CELLS:]], axis=0)
    pieces = split(field, 3)
    times = pos_ref.shape[1]
    cell = lax.broadcasted_iota(jnp.int32, (CELLS, STEP), 0)
    for begin in range(0, times, STEP):
        onehot = jnp.where(cell == pos_ref[:, begin : begin + STEP], 1.0, 0.0).astype(jnp.bfloat16)
        total = jnp.dot(pieces[0], onehot, preferred_element_type=jnp.float32)
        for piece in pieces[1:]:
            total = total + jnp.dot(piece, onehot, preferred_element_type=jnp.float32)
        out_ref[:, begin : begin + STEP] = total


def tables(weight, positions, scale):
    times = positions.shape[0]
    return pl.pallas_call(
        functools.partial(tables_kernel, scale),
        out_shape=jax.ShapeDtypeStruct((2 * ZERN, times), jnp.float32),
        name="projection_per_sample",
        compiler_params=pltpu.CompilerParams(vmem_limit_bytes=12 * 2**20),
        cost_estimate=pl.CostEstimate(flops=4_000_000_000, bytes_accessed=2_000_000, transcendentals=0),
    )(weight.reshape(1, CELLS), jnp.asarray(zernike_rows()), jnp.asarray(dft_rows()), positions.reshape(1, times))


def inverse_kernel(weight_ref, zern_ref, out_ref):
    zern = zern_ref[...]
    gram = lax.dot_general(
        zern * weight_ref[...], zern, ROWS, precision=HIGHEST, preferred_element_type=jnp.float32
    )
    inverse = invert(gram)
    zeros = jnp.zeros_like(inverse)
    inverse = jnp.concatenate(
        [jnp.concatenate([inverse, zeros], axis=1), jnp.concatenate([zeros, inverse], axis=1)], axis=0
    )
    high, low = split(inverse, 2)
    out_ref[...] = jnp.concatenate([high, high, low], axis=0)


def gram_inverse(weight):
    return pl.pallas_call(
        inverse_kernel,
        out_shape=jax.ShapeDtypeStruct((6 * ZERN, 2 * ZERN), jnp.bfloat16),
        name="gram_inverse",
        compiler_params=pltpu.CompilerParams(vmem_limit_bytes=4 * 2**20),
        cost_estimate=pl.CostEstimate(flops=5_000_000_000, bytes_accessed=200_000, transcendentals=0),
    )(weight.reshape(1, CELLS), jnp.asarray(zernike_rows()))


def shift_order(stat_count):
    return [0, 2, 3, 1] if stat_count == 4 else list(range(stat_count))


def correlate_kernel(owners, stat_count, index_ref, volt_ref, *args):
    part_refs, args = args[:stat_count], args[stat_count:]
    extra_ref, table_ref, *out_refs = args[:-7]
    refs_ref, left_a, left_b, total_ref, stage_ref, more_ref, more_sem = args[-7:]
    chans, parts, stations, times = volt_ref.shape
    refs = index_ref.shape[0]
    count = refs // 2
    steps = times // STEP
    me = lax.axis_index("stat")
    places, more = [], jnp.int32(0)
    for owner, slot in zip(*owner_and_slot(index_ref, stations)):
        shift, place = jnp.bitwise_xor(me, owner), jnp.int32(0)
        for i, k in enumerate(shift_order(stat_count)):
            place = jnp.where(shift == k, i, place)
        places.append(((slot // count) * stat_count + place, lax.rem(slot, count)))
        more = more + slot // count
    for i, part_ref in enumerate(part_refs):
        refs_ref[i] = part_ref[...].astype(jnp.float32)

    @pl.when(more > 0)
    def _():
        copy = pltpu.make_async_copy(extra_ref, more_ref, more_sem)
        copy.start()
        copy.wait()
        for i in range(stat_count):
            refs_ref[stat_count + i] = more_ref[i].astype(jnp.float32)

    own = stations // (len(owners) if owners else 1)
    begins = [0]
    if owners:
        tm, chan_at, chan_count = lax.axis_index("tm"), lax.axis_index("chan"), lax.axis_size("chan")
        begins = [
            pl.multiple_of(
                (jnp.bitwise_xor(tm, dt) * chan_count + jnp.bitwise_xor(chan_at, dc)) * own, own
            )
            for dt, dc in owners
        ]

    def produce(chan, step, left_ref):
        span = pl.ds(step * STEP, STEP)
        for r, (place, row) in enumerate(places):
            real = refs_ref[place, chan, pl.ds(row, 1), span]
            imag = refs_ref[place, chan, pl.ds(count + row, 1), span]
            for half in range(0, ZERN, 16):
                table_r = table_ref[half : half + 16, span]
                table_i = table_ref[ZERN + half : ZERN + half + 16, span]
                for at, value in (
                    (half, real * table_r + imag * table_i),
                    (ZERN + half, real * table_i - imag * table_r),
                ):
                    high, low = split(value, 2)
                    left_ref[pl.ds(r * 2 * ZERN + at, 16), :] = high
                    left_ref[pl.ds((refs + r) * 2 * ZERN + at, 16), :] = low

    def consume(chan, step, left_ref):
        span = pl.ds(step * STEP, STEP)
        right = jnp.concatenate(
            [volt_ref[chan, k, pl.ds(begin, own), span] for k in range(parts) for begin in begins], axis=0
        )
        product = lax.dot_general(left_ref[...], right, ROWS, preferred_element_type=jnp.float32)
        product = product[: refs * 2 * ZERN] + product[refs * 2 * ZERN :]
        if step == 0:
            total_ref[...] = product
        else:
            total_ref[...] += product

    def finish(chan):
        kept = lax.broadcasted_iota(jnp.int32, (1, stations), 1) < own
        levels = []
        for r in range(refs):
            top = total_ref[r * 2 * ZERN : r * 2 * ZERN + ZERN, :]
            low = total_ref[r * 2 * ZERN + ZERN : (r + 1) * 2 * ZERN, :]
            real = top[:, :stations] - low[:, stations:]
            imag = top[:, stations:] + low[:, :stations]
            both = jnp.concatenate([real, imag], axis=0)
            if owners:
                most = jnp.maximum(jnp.max(jnp.abs(both), axis=0, keepdims=True), 1e-30)
                level = jnp.floor(jnp.log2(most) * LEVELS) + 1.0
                levels.append(level)
                rounded = jnp.floor(both * (jnp.exp2(level * (-1.0 / LEVELS)) * MOST) + 0.5)
                both = jnp.where(kept, both, rounded)
            stage_ref[pl.ds(r, stations, stride=refs), :] = both.T
        if not owners:
            out_refs[0][chan] = stage_ref[: stations * refs, :]
            return
        rows = own * refs
        out_refs[0][chan] = stage_ref[:rows, :]
        level = jnp.concatenate(levels, axis=0).astype(jnp.int32).astype(jnp.int16)
        for i, out_ref in enumerate(out_refs[1:]):
            block = stage_ref[(i + 1) * rows : (i + 2) * rows, :]
            out_ref[chan * rows : (chan + 1) * rows, :] = block.astype(jnp.int32).astype(jnp.int16)
            out_ref[chans * rows + chan * refs : chans * rows + (chan + 1) * refs, :] = level

    order = [(chan, step) for chan in range(chans) for step in range(steps)]
    buffers = (left_a, left_b)
    produce(*order[0], buffers[0])
    for i, (chan, step) in enumerate(order):
        if i + 1 < len(order):
            produce(*order[i + 1], buffers[(i + 1) % 2])
        consume(chan, step, buffers[i % 2])
        if step == steps - 1:
            finish(chan)


def correlate(ref_index, voltages, ref_parts, extra, table, owners):
    chans, parts, stations, times = voltages.shape
    refs = ref_index.shape[0]
    vmem = pl.BlockSpec(memory_space=pltpu.VMEM)
    rows = stations // (len(owners) if owners else 1) * refs
    shapes = [jax.ShapeDtypeStruct((chans, rows, 2 * ZERN), jnp.float32)]
    if owners:
        shapes += [jax.ShapeDtypeStruct((chans * (rows + refs), 2 * ZERN), jnp.int16)] * (len(owners) - 1)
    return pl.pallas_call(
        functools.partial(correlate_kernel, owners, len(ref_parts)),
        in_specs=[pl.BlockSpec(memory_space=pltpu.SMEM)]
        + [vmem] * (1 + len(ref_parts))
        + [pl.BlockSpec(memory_space=pltpu.HBM), vmem],
        out_specs=[vmem] * len(shapes),
        out_shape=shapes,
        scratch_shapes=[
            pltpu.VMEM((2 * len(ref_parts),) + ref_parts[0].shape, jnp.float32),
            pltpu.VMEM((2 * refs * 2 * ZERN, STEP), jnp.bfloat16),
            pltpu.VMEM((2 * refs * 2 * ZERN, STEP), jnp.bfloat16),
            pltpu.VMEM((refs * 2 * ZERN, parts * stations), jnp.float32),
            pltpu.VMEM(((stations + 1) * refs, 2 * ZERN), jnp.float32),
            pltpu.VMEM(extra.shape, extra.dtype),
            pltpu.SemaphoreType.DMA,
        ],
        compiler_params=pltpu.CompilerParams(vmem_limit_bytes=24 * 2**20),
        cost_estimate=pl.CostEstimate(flops=8_600_000_000, bytes_accessed=5_000_000, transcendentals=0),
        name="correlate",
    )(ref_index, voltages, *ref_parts, pltpu.with_memory_space_constraint(extra, pltpu.HBM), table)


def unwritten(shape, dtype):
    return pl.pallas_call(
        lambda out_ref: None,
        out_specs=pl.BlockSpec(memory_space=pltpu.HBM),
        out_shape=jax.ShapeDtypeStruct(shape, dtype),
        name="no_second_round",
    )()


def collect_kernel(order, shape, *refs):
    *ins, inverse_ref, out_ref, stage_ref, sems = refs
    ins = [ins[list(order).index(at)] for at in range(len(ins))]
    chan = lax.axis_index("chan")
    chan_count = lax.axis_size("chan")
    tm_count = len(ins) // chan_count
    chans, own, rows, terms = shape
    copies = []
    for dc in range(chan_count):
        source = jnp.bitwise_xor(chan, dc)
        for c in range(chans):
            total = None
            for at in range(dc, len(ins), chan_count):
                if ins[at].dtype == jnp.int16:
                    begin = c * own * rows
                    level = ins[at][chans * own * rows :, :].astype(jnp.int32).astype(jnp.float32)
                    step = jnp.exp2(level[c * rows : (c + 1) * rows] * (1.0 / LEVELS)) * (1.0 / MOST)
                    part = ins[at][begin : begin + own * rows, :].astype(jnp.int32).astype(jnp.float32)
                    steps = [step[:, at * own + s : at * own + s + 1] for s in range(own)]
                    steps = [jnp.broadcast_to(x, (rows, terms)) for x in steps]
                    part = part * jnp.concatenate(steps, axis=0)
                else:
                    part = ins[at][c].reshape(own * rows, terms)
                total = part if total is None else total + part
            high, low = split(total, 2)
            pieces = jnp.concatenate([high, low, high], axis=1)
            solved = jnp.dot(pieces, inverse_ref[...], preferred_element_type=jnp.float32)
            stage_ref[dc, :, c] = solved.reshape(own, rows, terms)
        to = out_ref.at[:, pl.ds(source * chans, chans)]
        copies.append(pltpu.make_async_copy(stage_ref.at[dc], to, sems.at[dc]))
        copies[-1].start()
    for copy in copies:
        copy.wait()


def collect(pieces, order, inverse, chan_count, shape):
    chans, stations, refs, terms = shape
    vmem = pl.BlockSpec(memory_space=pltpu.VMEM)
    return pl.pallas_call(
        functools.partial(collect_kernel, order, shape),
        in_specs=[vmem] * (len(pieces) + 1),
        out_specs=pl.BlockSpec(memory_space=pltpu.HBM),
        out_shape=jax.ShapeDtypeStruct((stations, chans * chan_count, refs, terms), jnp.float32),
        scratch_shapes=[
            pltpu.VMEM((chan_count, stations, chans, refs, terms), jnp.float32),
            pltpu.SemaphoreType.DMA((chan_count,)),
        ],
        compiler_params=pltpu.CompilerParams(vmem_limit_bytes=8 * 2**20),
        name="sum_and_solve",
    )(*pieces, inverse)


def on_device(voltages, ref_index, positions, aperture_weight):
    chans, parts, stations, times = voltages.shape
    refs = ref_index.shape[0]
    stat_count = lax.axis_size("stat")
    tm_count = lax.axis_size("tm")
    chan_count = lax.axis_size("chan")
    first, second = pick(ref_index, voltages)

    def to_all(own):
        shifts = [[(i, i ^ k) for i in range(stat_count)] for k in shift_order(stat_count)[1:]]
        return [own] + [lax.ppermute(own, "stat", pairs) for pairs in shifts]

    ref_parts = to_all(first)
    holders = ref_index // stations
    most = jnp.max(jnp.sum(holders[:, None] == jnp.arange(stat_count)[None, :], axis=0))
    second, *ref_parts = lax.optimization_barrier((second, *ref_parts))
    extra = lax.cond(
        most > refs // 2,
        lambda own: jnp.stack(to_all(own)),
        lambda own: unwritten((stat_count,) + own.shape, own.dtype),
        second,
    )
    scale = (tm_count * times / CELLS) ** (-0.5)
    table = tables(aperture_weight, positions, scale)
    inverse = gram_inverse(aperture_weight)
    owners = [(dt, dc) for dt in range(tm_count) for dc in range(chan_count)]
    order = [0, 4, 5, 2, 3, 1, 6, 7] if len(owners) == 8 else range(len(owners))
    own = stations // len(owners)
    block = (chans, own, refs, 2 * ZERN)
    if own % GROUP == 0:
        sums = correlate(ref_index, voltages, ref_parts, extra, table, owners)
    else:
        whole = correlate(ref_index, voltages, ref_parts, extra, table, None)[0]
        whole = whole.reshape((chans, len(owners)) + block[1:])
        tm, chan = lax.axis_index("tm"), lax.axis_index("chan")
        sums = [
            lax.dynamic_index_in_dim(whole, (tm ^ dt) * chan_count + (chan ^ dc), 1, keepdims=False)
            for dt, dc in owners
        ]
    pieces = []
    for at in order:
        x = sums[at]
        if at:
            dt, dc = owners[at]
            pairs = [
                (c * tm_count + t, (c ^ dc) * tm_count + (t ^ dt))
                for c in range(chan_count)
                for t in range(tm_count)
            ]
            x = lax.ppermute(x, ("chan", "tm"), pairs)
        pieces.append(x)
    return collect(pieces, order, inverse, chan_count, block)


def solution(mesh):
    in_specs = (P("chan", None, "stat", "tm"), P(), P("tm"), P())
    out_specs = P(("stat", "tm", "chan"), None, None, None)
    return jax.shard_map(
        on_device, mesh=mesh, in_specs=in_specs, out_specs=out_specs, check_vma=False
    )
```
